512 devices in a mesh: lat: 64 (over y, x, z_lo), lon: 8 (over z_hi, core).
Axes of the slice: x: 4, y: 8, z: 8 (z_hi: 4, z_lo: 2; z = z_hi * 2 + z_lo), core: 2. Of those that a mesh axis runs over, the one named last changes fastest.
Arguments:
- grid_state: bfloat16 [2, 384, 192, 192], P(None, 'lat', 'lon'), may hold values from -20 to 20
- cotangent: bfloat16 [2, 384, 192, 192], P(None, 'lat', 'lon'), may hold values from -6 to 6
- mask_ids: int32 [2, 384, 192], P(None, 'lat', 'lon'), may hold values from 0 to 2
- earth_bias: float32 [2, 6, 12, 12, 23], replicated, may hold values from -6 to 360
- qkv_weight: bfloat16 [192, 576], replicated, may hold values from -0.4375 to 0.4375
- proj_weight: bfloat16 [192, 192], replicated, may hold values from -0.4375 to 0.4375
Outputs:
- grad_field: bfloat16 [2, 384, 192, 192], P(None, 'lat', 'lon')
- grad_qkv: float32 [192, 576], replicated
- grad_proj: float32 [192, 192], replicated
- grad_bias: float32 [2, 6, 12, 12, 23], replicated
The draws below stay inside these ranges and needn't reach their ends.
Inputs may be any that keep to these rules, and one draw needn't show every extreme that they name: `mask_ids`: cells of different mask ids do not attend to each other.
All inputs are finite; a program needn't handle non-finite values.
Results may differ from the reference program's by a relative error of at most 0.011.
Values may be sent and summed in bfloat16 or wider, within the bound.
A program may use at most 64 MiB of HBM per device.

```python
import jax
import jax.numpy as jnp
from jax import lax

C = 192
HEADS = 6
LEVELS = 2
ROWS = 12
BANDS = 2
MEMBERS = 32
NLAT = 384
NLON = 192
TOKENS = 147456


def draw_grid_state(key, part):
    key = jax.random.fold_in(key, 11)
    shape = (LEVELS, NLAT, NLON, C)
    values = jnp.clip(jax.random.normal(key, shape, jnp.float32), -6.0, 6.0)
    return values.astype(jnp.bfloat16)


def draw_earth_bias(key, part):
    key = jax.random.fold_in(key, 23)
    shape = (BANDS, HEADS, 12, 12, 23)
    base = jnp.clip(jax.random.normal(key, shape, jnp.float32), -6.0, 6.0)
    return base


def set_ends(entries, rng, low, high):
    index_at = [jax.random.randint(jax.random.fold_in(rng, axis), (), 0, length) for axis, length in enumerate(entries.shape)]
    longest = entries.shape.index(max(entries.shape))
    next_to = index_at[:longest] + [(index_at[longest] + 1) % entries.shape[longest]] + index_at[longest + 1:]
    return entries.at[tuple(index_at)].set(low).at[tuple(next_to)].set(high)


def steps_of(key, extent, cuts, least, largest):
    def one(position, shards_of):
        steps = jax.random.uniform(jax.random.fold_in(jax.random.fold_in(key, 6), position), (shards_of,), jnp.float32, least / len(cuts), largest / len(cuts))
        return jnp.repeat(jnp.exp(steps), extent[position] // shards_of).reshape((-1,) + (1,) * (len(extent) - position - 1))

    loudness = one(*cuts[0])
    for cut in cuts[1:]:
        loudness = loudness * one(*cut)
    return loudness


def noise(key, dims, scale, most, pieces=(), kind=jnp.bfloat16):
    loudness = steps_of(key, dims, pieces, -0.22, 0.18) if pieces else 1.0
    result = jax.random.normal(key, dims, jnp.float32) * scale * loudness
    return jnp.minimum(jnp.maximum(result, -most), most).astype(kind)


def setup_inputs(seed: int = 0) -> dict:
    arg_keys = jax.random.split(jax.random.key(seed), 7)
    grid_state = draw_grid_state(jax.random.fold_in(arg_keys[6], 71), 0)
    cotangent = noise(arg_keys[1], (LEVELS, NLAT, NLON, C), 1.0, 6.0, ((1, 64), (2, 8)))
    mask_ids = set_ends(jax.random.randint(arg_keys[2], (LEVELS, NLAT, NLON), 0, 3), jax.random.fold_in(arg_keys[2], 1), 0, 2).astype(jnp.int32)
    earth_bias = draw_earth_bias(jax.random.fold_in(arg_keys[6], 71), 0)
    qkv_weight = noise(arg_keys[4], (C, 3 * C), C ** -0.5, 0.4375)
    proj_weight = noise(arg_keys[5], (C, C), C ** -0.5, 0.4375)
    return dict(grid_state=grid_state, cotangent=cotangent, mask_ids=mask_ids, earth_bias=earth_bias, qkv_weight=qkv_weight, proj_weight=proj_weight)


def offset_table():
    places = jnp.arange(12, dtype=jnp.int32)
    spread = places[:, None] - places[None, :] + 11
    return (spread[:, :, None] == jnp.arange(23, dtype=jnp.int32)[None, None, :]).astype(jnp.float32)

def window_grad(grid_block, cot_block, id_block, region, bias_block, qkv_weight, proj_weight, offsets):
    levels, rows_dev, cols_dev, width = grid_block.shape
    lat_windows = rows_dev // 6
    longitude_window_count = cols_dev // 12
    head_count = bias_block.shape[1]
    head_size = width // head_count
    win_size = levels * 72
    score_scale = head_size ** (-0.5)

    def to_windows(tensor):
        last_dim = tensor.shape[-1]
        shaped = tensor.reshape(levels, lat_windows, 6, longitude_window_count, 12, last_dim)
        return shaped.transpose(1, 3, 0, 2, 4, 5).reshape(lat_windows, longitude_window_count, win_size, last_dim)

    def from_windows(tensor):
        last_dim = tensor.shape[-1]
        shaped = tensor.reshape(lat_windows, longitude_window_count, levels, 6, 12, last_dim)
        return shaped.transpose(2, 0, 3, 1, 4, 5).reshape(levels * rows_dev * cols_dev, last_dim)
    inputs = grid_block.astype(jnp.float32).reshape(-1, width)
    mean_removed = inputs - lax.optimization_barrier(jnp.mean(inputs, axis=-1, keepdims=True))
    reciprocal_deviation = lax.rsqrt(lax.optimization_barrier(jnp.mean(mean_removed * mean_removed, axis=-1, keepdims=True)) + 1e-05)
    standardized_input = mean_removed * reciprocal_deviation
    normalized_input = standardized_input.astype(jnp.bfloat16)
    projected = jnp.dot(normalized_input, qkv_weight, preferred_element_type=jnp.float32).astype(jnp.bfloat16)
    split_win = to_windows(projected).reshape(lat_windows, longitude_window_count, win_size, 3, head_count, head_size)
    queries = split_win[:, :, :, 0]
    keys_win = split_win[:, :, :, 1]
    values_win = split_win[:, :, :, 2]
    full_bias = jnp.einsum('rhabo,xyo->rhaxby', bias_block, offsets, precision=lax.Precision.HIGHEST)
    full_bias = full_bias.reshape(lat_windows, head_count, win_size, win_size)
    id_win = to_windows(id_block.reshape(-1, 1))[..., 0]
    region_tok = jnp.broadcast_to(region[None, :, None], (levels, rows_dev, cols_dev)).reshape(-1, 1)
    region_win = to_windows(region_tok)[..., 0]
    allowed = (id_win[..., :, None] == id_win[..., None, :]) & (region_win[..., :, None] == region_win[..., None, :])
    scores = jnp.einsum('rnqhd,rnkhd->rnhqk', queries.astype(jnp.float32), keys_win.astype(jnp.float32)) * score_scale
    scores = scores + full_bias[:, None]
    scores = jnp.where(allowed[:, :, None], scores, -jnp.inf)
    row_max = lax.optimization_barrier(jnp.max(scores, axis=-1, keepdims=True))
    exponent = jnp.exp(scores - row_max)
    softmaxed = exponent / lax.optimization_barrier(jnp.sum(exponent, axis=-1, keepdims=True))
    soft_bf = softmaxed.astype(jnp.bfloat16)
    attended = jnp.einsum('rnhqk,rnkhd->rnqhd', soft_bf.astype(jnp.float32), values_win.astype(jnp.float32)).astype(jnp.bfloat16)
    att_tokens = from_windows(attended.reshape(lat_windows, longitude_window_count, win_size, width))
    cot_tokens = cot_block.reshape(-1, width)
    grad_proj = jnp.dot(att_tokens.T, cot_tokens, preferred_element_type=jnp.float32)
    d_att = jnp.dot(cot_tokens, proj_weight.T, preferred_element_type=jnp.float32).astype(jnp.bfloat16)
    d_att = to_windows(d_att).reshape(lat_windows, longitude_window_count, win_size, head_count, head_size)
    d_value = jnp.einsum('rnhqk,rnqhd->rnkhd', soft_bf.astype(jnp.float32), d_att.astype(jnp.float32)).astype(jnp.bfloat16)
    d_prob = jnp.einsum('rnqhd,rnkhd->rnhqk', d_att.astype(jnp.float32), values_win.astype(jnp.float32))
    d_score = softmaxed * (d_prob - lax.optimization_barrier(jnp.sum(softmaxed * d_prob, axis=-1, keepdims=True)))
    band_sum = lax.optimization_barrier(jnp.sum(d_score, axis=1)).reshape(lat_windows, head_count, levels * 6, 12, levels * 6, 12)
    grad_bias = jnp.einsum('rhaxby,xyo->rhabo', band_sum, offsets, precision=lax.Precision.HIGHEST)
    score_bf = d_score.astype(jnp.bfloat16)
    d_query = (jnp.einsum('rnhqk,rnkhd->rnqhd', score_bf.astype(jnp.float32), keys_win.astype(jnp.float32)) * score_scale).astype(jnp.bfloat16)
    d_key = (jnp.einsum('rnhqk,rnqhd->rnkhd', score_bf.astype(jnp.float32), queries.astype(jnp.float32)) * score_scale).astype(jnp.bfloat16)
    d_qkv = jnp.stack([d_query, d_key, d_value], axis=3).reshape(lat_windows, longitude_window_count, win_size, 3 * width)
    d_qkv = from_windows(d_qkv)
    grad_qkv = jnp.dot(normalized_input.T, d_qkv, preferred_element_type=jnp.float32)
    normalized_gradient = jnp.dot(d_qkv, qkv_weight.T, preferred_element_type=jnp.float32)
    mean_removed_gradient = normalized_gradient - lax.optimization_barrier(jnp.mean(normalized_gradient, axis=-1, keepdims=True)) - standardized_input * lax.optimization_barrier(jnp.mean(normalized_gradient * standardized_input, axis=-1, keepdims=True))
    grad_field = cot_tokens.astype(jnp.float32) + reciprocal_deviation * mean_removed_gradient
    return (grad_field.astype(jnp.bfloat16).reshape(grid_block.shape), grad_qkv, grad_proj, grad_bias)

def member_grad(grid_m, cot_m, ids_m, earth_bias, qkv_weight, proj_weight, offsets):
    levels, lat_total, lon_total, width = grid_m.shape

    def band_step(carry, band):
        row_index = (6 * band + 3 + jnp.arange(6, dtype=jnp.int32)) % lat_total
        region = (6 * band + 3 + jnp.arange(6, dtype=jnp.int32) >= lat_total).astype(jnp.int32)

        def pick(tensor):
            return jnp.roll(jnp.take(tensor, row_index, axis=1), -6, axis=2)
        bias_band = lax.dynamic_slice_in_dim(earth_bias, band, 1, 0)
        grad_band, part_qkv, part_proj, part_bias = window_grad(pick(grid_m), pick(cot_m), pick(ids_m), region, bias_band, qkv_weight, proj_weight, offsets)
        return ((carry[0] + part_qkv, carry[1] + part_proj), (jnp.roll(grad_band, 6, axis=2), part_bias[0]))
    start = (jnp.zeros((width, 3 * width), jnp.float32), jnp.zeros((width, width), jnp.float32))
    sums, stacked = lax.scan(band_step, start, jnp.arange(lat_total // 6, dtype=jnp.int32))
    bands, grad_bias = stacked
    grad_field = bands.transpose(1, 0, 2, 3, 4).reshape(levels, lat_total, lon_total, width)
    grad_field = jnp.roll(grad_field, 3, axis=1)
    return (grad_field, sums[0], sums[1], grad_bias)

def reference(grid_state, cotangent, mask_ids, earth_bias, qkv_weight, proj_weight):
    levels, lat_all, lon_total, width = grid_state.shape
    offsets = offset_table()

    def member_step(carry, member):
        first_row = (member * ROWS).astype(jnp.int32)
        grid_m = lax.dynamic_slice_in_dim(grid_state, first_row, ROWS, 1)
        cot_m = lax.dynamic_slice_in_dim(cotangent, first_row, ROWS, 1)
        ids_m = lax.dynamic_slice_in_dim(mask_ids, first_row, ROWS, 1)
        field_m, part_qkv, part_proj, part_bias = member_grad(grid_m, cot_m, ids_m, earth_bias, qkv_weight, proj_weight, offsets)
        return ((carry[0] + part_qkv, carry[1] + part_proj, carry[2] + part_bias), field_m)
    start = (jnp.zeros((width, 3 * width), jnp.float32), jnp.zeros((width, width), jnp.float32), jnp.zeros(earth_bias.shape, jnp.float32))
    sums, fields = lax.scan(member_step, start, jnp.arange(MEMBERS, dtype=jnp.int32))
    grad_field = fields.transpose(1, 0, 2, 3, 4).reshape(levels, lat_all, lon_total, width)
    token_scale = TOKENS ** (-0.5)
    return (grad_field, sums[0] * token_scale, sums[1] * token_scale, sums[2])
```

```python
import functools

import jax
import jax.numpy as jnp
import numpy as np
from jax import lax
from jax.experimental import pallas as pl
from jax.experimental.pallas import tpu as pltpu
from jax.sharding import PartitionSpec as P

MESH = pl.DeviceIdType.MESH
F32, BF16 = jnp.float32, jnp.bfloat16

TOK = 288
WIN = 144
WIDTH = 192
HEADS = 6
OWN, EAST, SWAP, CORNER, ALL = 0, 288, 336, 448, 496
CHUNKS, TILES = 8, 7
HALF = 51
ROWS_MAIN, COLS_MAIN = 12, 6
BIAS_TILES = 15


def build_tables():
    natural = lambda z, r, c: (z * 6 + r) * 24 + c
    send = np.zeros((208, TOK), np.float32)
    for z in range(2):
        for r in range(3):
            for c in range(6):
                send[(z * 3 + r) * 6 + c, natural(z, r + 3, c)] = 1
                send[160 + (z * 3 + r) * 6 + c, natural(z, r, c)] = 1
            for c in range(18):
                send[48 + (z * 3 + r) * 18 + c, natural(z, r, c + 6)] = 1
    frame = np.zeros((TOK, ALL), np.float32)
    id_rows = np.zeros((TOK, 64), np.float32)
    id_cols = np.zeros((TOK, 128), np.float32)
    wrapped = np.zeros((TOK, 128), np.float32)
    for w in range(2):
        for z in range(2):
            for r in range(6):
                for p in range(12):
                    t = w * WIN + (z * 6 + r) * 12 + p
                    c = w * 12 + p
                    if r < 3 and c < 18:
                        src, block, row, col = natural(z, r + 3, c + 6), 0, r + 3, c + 6
                    elif r < 3:
                        src, block, row, col = EAST + (z * 3 + r) * 6 + c - 18, 1, r + 3, c - 18
                    elif c < 18:
                        src, block, row, col = SWAP + (z * 3 + r - 3) * 18 + c, 2, r - 3, c + 6
                    else:
                        src, block, row, col = (
                            CORNER + (z * 3 + r - 3) * 6 + c - 18, 3, r - 3, c - 18)
                    frame[t, src] = 1
                    id_rows[t, block * 16 + z * 8 + row] = 1
                    id_cols[t, col] = 1
                    wrapped[t, :] = 3.0 if r >= 3 else 0.0
    back = frame[:, OWN + TOK:].T
    out = np.concatenate([frame[:, :TOK].T, send.T], axis=1)
    spread = np.zeros((384, 1792), np.float32)
    for x in range(12):
        for b in range(12):
            for y in range(12):
                key = b * 12 + y
                col = x * 128 + key if key < 128 else 1536 + x * 16 + key - 128
                spread[b * 32 + x - y + 11, col] = 1
    cells = np.concatenate([send, back], axis=0)
    moves = np.concatenate([frame, out], axis=0)
    ids = np.concatenate([id_rows, np.zeros((TOK, 64), np.float32), id_cols, wrapped], axis=1)
    return [np.asarray(t, jnp.bfloat16) for t in (cells, moves, ids, spread)]


def mm(a, b):
    return lax.dot_general(a, b, (((1,), (0,)), ((), ())), preferred_element_type=F32)


def mm_nt(a, b):
    return lax.dot_general(a, b, (((1,), (1,)), ((), ())), preferred_element_type=F32)


def mm_tn(a, b):
    return lax.dot_general(a, b, (((0,), (0,)), ((), ())), preferred_element_type=F32)


def tile_place(t):
    return t // HALF, (t % HALF) // TILES, (t % HALF) % TILES


def kernel(
    x_hbm, cot_hbm, ids_hbm, eb_hbm, wqkv_hbm, wproj_hbm, cells_hbm, moves_hbm, idt_hbm, spread_hbm,
    field_ref, gqkv_ref, gproj_ref, gbias_ref,
    x_v, cot_v, ids_v, eb_v, wqkv_v, wproj_v, cells_v, moves_v, idt_v, spread_v,
    xc, send_b, idb, e2d, fa, fb, ba, bb, gback, ret_b, gs,
    pay, rc, cur, ra, ry, rz, fin, o2d,
    in_sem, h_ss, h_rs, r_ss, r_rs, c_ss, c_rs, a_ss, a_rs, y_ss, y_rs, z_ss, z_rs,
    g_ss, g_rs, k_ss, k_rs,
):
    lat, lon = lax.axis_index("lat"), lax.axis_index("lon")
    iy, ix, izl = lat // 8, (lat // 2) % 4, lat % 2
    izh, core = lon // 2, lon % 2
    group = ix * 2 + izl
    band = izl

    lat_o = lat + 1 - 2 * izl
    east, west = (lon + 1) % 8, (lon + 7) % 8
    sibling = (lat, izh * 2 + 1 - core)

    def member(g):
        return (iy * 8 + g, lon)

    def at_y(y):
        return (y * 8 + group, lon)

    def at_zh(zh):
        return (lat, zh * 2 + core)

    barrier = pltpu.get_barrier_semaphore()
    partners = [(lat, west), (lat, east), (lat_o, lon), (lat_o, west), (lat_o, east), sibling]
    partners += [member((group + d) % 8) for d in range(1, 8)]
    partners += [at_y((iy + d) % 8) for d in range(1, 8)]
    partners += [at_zh((izh + d) % 4) for d in range(1, 4)]
    for p in partners:
        pl.semaphore_signal(barrier, inc=1, device_id=p, device_id_type=MESH)

    srcs = [x_hbm, cot_hbm, cells_hbm, ids_hbm, eb_hbm.at[band], spread_hbm, moves_hbm, idt_hbm,
            wqkv_hbm, wproj_hbm]
    dsts = [x_v, cot_v, cells_v, ids_v, eb_v, spread_v, moves_v, idt_v, wqkv_v, wproj_v]
    loads = [pltpu.make_async_copy(s, d, in_sem.at[i]) for i, (s, d) in enumerate(zip(srcs, dsts))]
    for cp in loads:
        cp.start()

    loads[0].wait()
    loads[1].wait()
    loads[2].wait()
    loads[3].wait()
    xc[0:TOK, 0:192] = x_v[...]
    xc[0:TOK, 192:384] = cot_v[...]
    send_b[...] = mm(cells_v[0:208, :], xc[0:TOK, :]).astype(BF16)
    idb[0] = jnp.zeros((16, 128), F32)
    idb[0, 0:6, 0:24] = ids_v[0].astype(F32)
    idb[0, 8:14, 0:24] = ids_v[1].astype(F32)

    pl.semaphore_wait(barrier, len(partners))

    def remote(src, dst, ss, rs, dev):
        return pltpu.make_async_remote_copy(
            src_ref=src, dst_ref=dst, send_sem=ss, recv_sem=rs, device_id=dev, device_id_type=MESH)

    strips = [(0, EAST, 48, (lat, west)), (48, SWAP, 112, (lat_o, lon)), (160, CORNER, 48, (lat_o, west))]
    halo = []
    for i, (a, b, n, dev) in enumerate(strips):
        halo.append(remote(send_b.at[pl.ds(a, n)], xc.at[pl.ds(b, n)], h_ss.at[i], h_rs.at[i], dev))
        halo.append(remote(idb.at[0], idb.at[i + 1], h_ss.at[3 + i], h_rs.at[3 + i], dev))
    for cp in halo:
        cp.start()

    loads[4].wait()
    loads[5].wait()
    e2d[...] = jnp.zeros(e2d.shape, F32)
    for h in range(HEADS):
        for a in range(12):
            r0 = (h * 12 + a) * 16
            e2d[r0:r0 + 12, 0:23] = eb_v[h, a]
    packs = []
    for g in range(3):
        acc = e2d[pl.ds(4 * g, 72, stride=16), :]
        for k in range(1, 4):
            acc = acc + pltpu.roll(e2d[pl.ds(4 * g + k, 72, stride=16), :], 32 * k, 1)
        packs.append(acc)
    e = jnp.concatenate(packs, axis=1)
    hi = e.astype(BF16)
    rest = e - hi.astype(F32)
    mid = rest.astype(BF16)
    low = (rest - mid.astype(F32)).astype(BF16)
    full = (mm(hi, spread_v[...]) + mm(mid, spread_v[...])) + mm(low, spread_v[...])
    for x in range(12):
        fa[pl.ds(x, 72, stride=12), :] = full[:, x * 128:(x + 1) * 128]
        tail = full[:, 1536 + (x // 8) * 128:1664 + (x // 8) * 128]
        shift = (128 - (x % 8) * 16) % 128
        fb[pl.ds(x, 72, stride=12), :] = pltpu.roll(tail, shift, 1) if shift else tail

    for cp in loads[6:]:
        cp.wait()
    for cp in halo:
        cp.wait_recv()

    fr = mm(moves_v[0:TOK, :], xc[...])
    xf = fr[:, 0:192]
    cot_f = fr[:, 192:384]
    cot = cot_f.astype(BF16)
    mean = jnp.sum(xf, axis=1, keepdims=True) * (1.0 / WIDTH)
    xm = xf - mean
    var = jnp.sum(xm * xm, axis=1, keepdims=True) * (1.0 / WIDTH)
    rdev = lax.rsqrt(var + 1e-05)
    xhat = xm * rdev
    normed = xhat.astype(BF16)
    wq, wk, wv = wqkv_v[:, 0:192], wqkv_v[:, 192:384], wqkv_v[:, 384:576]
    q = mm(normed, wq).astype(BF16)
    k = mm(normed, wk).astype(BF16)
    v = mm(normed, wv).astype(BF16)
    da = mm_nt(cot, wproj_v[...]).astype(BF16)

    id_all = jnp.concatenate([idb[i] for i in range(4)], axis=0).astype(BF16)
    id_row = mm(idt_v[:, 0:64], id_all) * idt_v[:, 128:256].astype(F32)
    id_cell = mm(id_row.astype(BF16), jnp.ones((128, 128), BF16))
    key = id_cell + idt_v[:, 256:384].astype(F32) * izl.astype(F32)
    classes = lax.broadcasted_iota(jnp.int32, (TOK, 128), 1).astype(F32)
    onehot = jnp.where(key == classes, 1.0, 0.0).astype(BF16)

    lane_head = lax.broadcasted_iota(jnp.int32, (WIN, WIDTH), 1) // 32
    scale = 32.0 ** (-0.5)
    atts, dqs, dks, dvs = [], [], [], []
    for w in range(2):
        rows = slice(w * WIN, (w + 1) * WIN)
        qw, kw, vw, daw = q[rows], k[rows], v[rows], da[rows]
        block = (mm_nt(onehot[rows], onehot[rows]) - 1.0) * 1e30
        att = dq = dk = dv = None
        for h in range(HEADS):
            here = lane_head == h
            zero = jnp.zeros((WIN, WIDTH), BF16)
            qh = jnp.where(here, qw, zero)
            kh = jnp.where(here, kw, zero)
            vh = jnp.where(here, vw, zero)
            dah = jnp.where(here, daw, zero)
            hr = slice(h * WIN, (h + 1) * WIN)
            bias = jnp.concatenate([fa[hr, :], fb[hr, 0:16]], axis=1)
            s = mm_nt(qh, kw) * scale + bias + block
            ex = jnp.exp(s - jnp.max(s, axis=1, keepdims=True))
            p = ex / jnp.sum(ex, axis=1, keepdims=True)
            pb = p.astype(BF16)
            dp = mm_nt(dah, vw)
            ds = p * (dp - jnp.sum(p * dp, axis=1, keepdims=True))
            dsb = ds.astype(BF16)
            ds_a = ds[:, 0:128]
            ds_b = jnp.concatenate([ds[:, 128:144], jnp.zeros((WIN, 112), F32)], axis=1)
            if w == 0:
                ba[hr, :] = ds_a
                bb[hr, :] = ds_b
            else:
                ba[hr, :] += ds_a
                bb[hr, :] += ds_b
            terms = (mm(pb, vh), mm(dsb, kh), mm_tn(dsb, qh), mm_tn(pb, dah))
            if h == 0:
                att, dq, dk, dv = terms
            else:
                att, dq, dk, dv = att + terms[0], dq + terms[1], dk + terms[2], dv + terms[3]
        atts.append(att.astype(BF16))
        dqs.append((dq * scale).astype(BF16))
        dks.append((dk * scale).astype(BF16))
        dvs.append(dv.astype(BF16))
    att = jnp.concatenate(atts, axis=0)
    dq = jnp.concatenate(dqs, axis=0)
    dk = jnp.concatenate(dks, axis=0)
    dv = jnp.concatenate(dvs, axis=0)

    gs[:, 0:192] = mm_tn(normed, dq)
    gs[:, 192:384] = mm_tn(normed, dk)
    gs[:, 384:576] = mm_tn(normed, dv)
    gs[:, 576:768] = mm_tn(att, cot)
    for i in range(ROWS_MAIN):
        for j in range(COLS_MAIN):
            pay[tile_place(i * COLS_MAIN + j)] = gs[
                i * 16:(i + 1) * 16, j * 128:(j + 1) * 128].astype(BF16)
    mains, tails = [], [None, None]
    for x in range(12):
        mains.append(ba[pl.ds(x, 72, stride=12), :])
        t = bb[pl.ds(x, 72, stride=12), :]
        if x % 8:
            t = pltpu.roll(t, (x % 8) * 16, 1)
        tails[x // 8] = t if tails[x // 8] is None else tails[x // 8] + t
    terms = jnp.concatenate(mains + tails, axis=1)
    t_hi = terms.astype(BF16)
    t_lo = (terms - t_hi.astype(F32)).astype(BF16)
    gb = mm_nt(t_hi, spread_v[...]) + mm_nt(t_lo, spread_v[...])
    gb = jnp.concatenate([gb, jnp.zeros((8, 384), F32)], axis=0)
    for which in range(2):
        mine = jnp.where(band == which, gb, 0.0).astype(BF16)
        for i in range(5):
            for j in range(3):
                pay[tile_place(72 + which * BIAS_TILES + i * 3 + j)] = mine[
                    i * 16:(i + 1) * 16, j * 128:(j + 1) * 128]
    for half in range(2):
        for t in range(HALF, CHUNKS * TILES):
            pay[half, t // TILES, t % TILES] = jnp.zeros((16, 128), BF16)

    order = [(group + d) % 8 for d in range(1, 9)]
    cores = [remote(pay.at[1 - core, j], rc.at[j], c_ss.at[d], c_rs.at[d], sibling)
             for d, j in enumerate(order)]
    for cp in cores:
        cp.start()

    dn = mm_nt(dq, wq) + mm_nt(dk, wk) + mm_nt(dv, wv)
    m1 = jnp.sum(dn, axis=1, keepdims=True) * (1.0 / WIDTH)
    m2 = jnp.sum(dn * xhat, axis=1, keepdims=True) * (1.0 / WIDTH)
    gf = (cot_f + rdev * (dn - m1 - xhat * m2)).astype(BF16)
    gback[0:TOK, :] = gf
    ret_b[...] = mm(cells_v[208:416, :], gf).astype(BF16)
    ret_to = [(lat, east), (lat_o, lon), (lat_o, east)]
    returns = [remote(ret_b.at[pl.ds(a, n)], gback.at[pl.ds(b, n)], r_ss.at[i], r_rs.at[i], ret_to[i])
               for i, (a, b, n, _) in enumerate(strips)]
    for cp in returns:
        cp.start()

    scatter = []
    for d, j in enumerate(order):
        cores[d].wait_recv()
        cur[j] = (pay[core, j].astype(F32) + rc[j].astype(F32)).astype(BF16)
        if d < 7:
            cp = remote(cur.at[j], ra.at[group], a_ss.at[d], a_rs.at[d], member(j))
            cp.start()
            scatter.append(cp)
    ra[group] = cur[group]

    for cp in returns:
        cp.wait_recv()
    field_ref[...] = mm(moves_v[TOK:2 * TOK, :], gback[...]).astype(BF16)

    def total(ref, n):
        acc = ref[0].astype(F32)
        for i in range(1, n):
            acc = acc + ref[i].astype(F32)
        return acc.astype(BF16)

    for cp in scatter:
        cp.wait_recv()
    ry[iy] = total(ra, 8)
    over_y = [remote(ry.at[iy], ry.at[iy], y_ss.at[d - 1], y_rs.at[d - 1], at_y((iy + d) % 8))
              for d in range(1, 8)]
    for cp in over_y:
        cp.start()
    for cp in over_y:
        cp.wait_recv()
    rz[izh] = total(ry, 8)
    over_z = [remote(rz.at[izh], rz.at[izh], z_ss.at[d - 1], z_rs.at[d - 1], at_zh((izh + d) % 4))
              for d in range(1, 4)]
    for cp in over_z:
        cp.start()
    for cp in over_z:
        cp.wait_recv()

    fin[core, group] = total(rz, 4)
    gather = [remote(fin.at[core, group], fin.at[core, group], g_ss.at[d - 1], g_rs.at[d - 1],
                     member((group + d) % 8)) for d in range(1, 8)]
    for cp in gather:
        cp.start()
    final = []
    for d in range(8):
        j = (group + 8 - d) % 8
        if d:
            gather[d - 1].wait_recv()
        cp = remote(fin.at[core, j], fin.at[core, j], k_ss.at[d], k_rs.at[d], sibling)
        cp.start()
        final.append(cp)
    for cp in final:
        cp.wait_recv()

    token_scale = 147456.0 ** (-0.5)
    for i in range(ROWS_MAIN):
        r = slice(i * 16, (i + 1) * 16)
        row = [fin[tile_place(i * COLS_MAIN + j)].astype(F32) * token_scale for j in range(COLS_MAIN)]
        for j in range(4):
            gqkv_ref[r, j * 128:(j + 1) * 128] = row[j]
        gqkv_ref[r, 512:576] = row[4][:, 0:64]
        gproj_ref[r, 0:64] = row[4][:, 64:128]
        gproj_ref[r, 64:192] = row[5]
    for which in range(2):
        for j in range(3):
            col = jnp.concatenate(
                [fin[tile_place(72 + which * BIAS_TILES + i * 3 + j)] for i in range(5)],
                axis=0).astype(F32)[0:72]
            for kk in range(4):
                part = pltpu.roll(col, 128 - 32 * kk, 1) if kk else col
                o2d[pl.ds(which * 1152 + 4 * j + kk, 72, stride=16), :] = part
        for h in range(HEADS):
            for a in range(12):
                r0 = which * 1152 + (h * 12 + a) * 16
                gbias_ref[which, h, a] = o2d[r0:r0 + 12, 0:23]

    for cp in halo + returns + cores + scatter + over_y + over_z + gather + final:
        cp.wait_send()


def body(grid_state, cotangent, mask_ids, earth_bias, qkv_weight, proj_weight):
    tables = [jnp.asarray(t) for t in build_tables()]
    vm = pltpu.VMEM
    dma = lambda n: pltpu.SemaphoreType.DMA((n,))
    scratch = [
        vm((TOK, WIDTH), BF16), vm((TOK, WIDTH), BF16), vm((2, 6, 24), jnp.int32),
        vm((6, 12, 12, 23), F32), vm((192, 576), BF16), vm((192, 192), BF16),
        vm((416, TOK), BF16), vm((576, ALL), BF16), vm((TOK, 384), BF16), vm((384, 1792), BF16),
        vm((ALL, 384), BF16), vm((208, 384), BF16), vm((4, 16, 128), F32), vm((1152, 128), F32),
        vm((864, 128), F32), vm((864, 128), F32), vm((864, 128), F32), vm((864, 128), F32),
        vm((ALL, WIDTH), BF16), vm((208, WIDTH), BF16), vm((192, 768), F32),
        vm((2, CHUNKS, TILES, 16, 128), BF16), vm((CHUNKS, TILES, 16, 128), BF16),
        vm((CHUNKS, TILES, 16, 128), BF16), vm((8, TILES, 16, 128), BF16),
        vm((8, TILES, 16, 128), BF16), vm((4, TILES, 16, 128), BF16),
        vm((2, CHUNKS, TILES, 16, 128), BF16), vm((2304, 128), F32),
        dma(10), dma(6), dma(6), dma(3), dma(3), dma(8), dma(8), dma(7), dma(7), dma(7), dma(7),
        dma(3), dma(3), dma(7), dma(7), dma(8), dma(8),
    ]
    any_space = pl.BlockSpec(memory_space=pl.ANY)
    in_vmem = pl.BlockSpec(memory_space=pltpu.VMEM)
    field, gqkv, gproj, gbias = pl.pallas_call(
        kernel,
        out_shape=(
            jax.ShapeDtypeStruct((TOK, WIDTH), BF16),
            jax.ShapeDtypeStruct((192, 576), F32),
            jax.ShapeDtypeStruct((192, 192), F32),
            jax.ShapeDtypeStruct((2, 6, 12, 12, 23), F32),
        ),
        in_specs=[any_space] * 10,
        out_specs=(in_vmem,) * 4,
        scratch_shapes=scratch,
        compiler_params=pltpu.CompilerParams(
            collective_id=0, has_side_effects=True, vmem_limit_bytes=48 * 2**20),
        name="window_backward",
    )(
        grid_state.reshape(TOK, WIDTH), cotangent.reshape(TOK, WIDTH), mask_ids, earth_bias,
        qkv_weight, proj_weight, *tables,
    )
    return field.reshape(grid_state.shape), gqkv, gproj, gbias


def solution(mesh):
    placed = (
        P(None, "lat", "lon", None),
        P(None, "lat", "lon", None),
        P(None, "lat", "lon"),
        P(),
        P(),
        P(),
    )
    return jax.shard_map(
        body,
        mesh=mesh,
        in_specs=placed,
        out_specs=(P(None, "lat", "lon", None), P(), P(), P()),
        check_vma=False,
    )
```

```python
import functools

import jax
import jax.numpy as jnp
import numpy as np
from jax import lax
from jax.experimental import pallas as pl
from jax.experimental.pallas import tpu as pltpu
from jax.sharding import PartitionSpec as P

MESH = pl.DeviceIdType.MESH
F32, BF16 = jnp.float32, jnp.bfloat16

TOK = 288
WIN = 144
WIDTH = 192
HEADS = 6
NEAR, FAR, EAST, CORNER, ALL = 288, 368, 416, 464, 512
STRIPS = ((0, NEAR, 80), (80, FAR, 48), (128, EAST, 48), (176, CORNER, 48))
SENT = 224
CHUNKS, TILES = 8, 7
MAIN, BIAS = 5, 2
HALF = 36
ROWS_MAIN, COLS_MAIN = 12, 6
BIAS_TILES = 15


def build_tables():
    natural = lambda z, r, c: (z * 6 + r) * 24 + c
    send = np.zeros((SENT, TOK), np.float32)
    for z in range(2):
        for r in range(3):
            row = z * 3 + r
            for c in range(12):
                send[row * 12 + c, natural(z, r, c + 6)] = 1
            for c in range(6):
                send[80 + row * 6 + c, natural(z, r, c + 18)] = 1
                send[128 + row * 6 + c, natural(z, r + 3, c)] = 1
                send[176 + row * 6 + c, natural(z, r, c)] = 1
    frame = np.zeros((TOK, ALL), np.float32)
    id_rows = np.zeros((TOK, 64), np.float32)
    id_cols = np.zeros((TOK, 128), np.float32)
    wrapped = np.zeros((TOK, 128), np.float32)
    for w in range(2):
        for z in range(2):
            for r in range(6):
                for p in range(12):
                    t = w * WIN + (z * 6 + r) * 12 + p
                    c = w * 12 + p
                    above = z * 3 + r - 3
                    if r < 3 and c < 18:
                        src, block, row, col = natural(z, r + 3, c + 6), 0, r + 3, c + 6
                    elif r < 3:
                        src, block, row, col = EAST + (z * 3 + r) * 6 + c - 18, 2, r + 3, c - 18
                    elif c < 12:
                        src, block, row, col = NEAR + above * 12 + c, 1, r - 3, c + 6
                    elif c < 18:
                        src, block, row, col = FAR + above * 6 + c - 12, 1, r - 3, c + 6
                    else:
                        src, block, row, col = CORNER + above * 6 + c - 18, 3, r - 3, c - 18
                    frame[t, src] = 1
                    id_rows[t, block * 16 + row * 2 + z] = 1
                    id_cols[t, col] = 1
                    wrapped[t, :] = 3.0 if r >= 3 else 0.0
    back = frame[:, TOK:].T
    out = np.concatenate([frame[:, :TOK].T, send.T], axis=1)
    spread = np.zeros((384, 1792), np.float32)
    for x in range(12):
        for b in range(12):
            for y in range(12):
                key = b * 12 + y
                col = x * 128 + key if key < 128 else 1536 + x * 16 + key - 128
                spread[b * 32 + x - y + 11, col] = 1
    cells = np.concatenate([send, back], axis=0)
    moves = np.concatenate([frame, out], axis=0)
    ids = np.concatenate([id_rows, np.zeros((TOK, 64), np.float32), id_cols, wrapped], axis=1)
    return [np.asarray(t, jnp.bfloat16) for t in (cells, moves, ids, spread)]


def mm(a, b):
    return lax.dot_general(a, b, (((1,), (0,)), ((), ())), preferred_element_type=F32)


def mm_nt(a, b):
    return lax.dot_general(a, b, (((1,), (1,)), ((), ())), preferred_element_type=F32)


def mm_tn(a, b):
    return lax.dot_general(a, b, (((0,), (0,)), ((), ())), preferred_element_type=F32)


def main_place(t):
    return t // HALF, (t % HALF) // MAIN, (t % HALF) % MAIN


def roll(a, shift):
    shift %= 128
    return pltpu.roll(a, shift, 1) if shift else a


def kernel(
    x_hbm, cot_hbm, ids_hbm, eb_hbm, wqkv_hbm, wproj_hbm, cells_hbm, moves_hbm, idt_hbm, spread_hbm,
    field_ref, fin,
    x_v, cot_v, ids_v, eb_v, wqkv_v, wproj_v, cells_v, moves_v, idt_v, spread_v,
    xc, send_b, idb, fa, fb, ba, bb, gback, ret_b, gs,
    pay_m, pay_b, rc_m, rc_b, cur, ra, ry, rz,
    in_sem, h_ss, h_rs, r_ss, r_rs, c_ss, c_rs, a_ss, a_rs, y_ss, y_rs, z_ss, z_rs,
    g_ss, g_rs, k_ss, k_rs,
):
    lat, lon = lax.axis_index("lat"), lax.axis_index("lon")
    iy, ix, izl = lat // 8, (lat // 2) % 4, lat % 2
    izh, core = lon // 2, lon % 2
    group = ix * 2 + izl
    band = izl

    lat_o = lat + 1 - 2 * izl
    east, west = (lon + 1) % 8, (lon + 7) % 8
    sibling = (lat, izh * 2 + 1 - core)

    def member(g):
        return (iy * 8 + g, lon)

    def at_y(y):
        return (y * 8 + group, lon)

    def at_zh(zh):
        return (lat, zh * 2 + core)

    barrier = pltpu.get_barrier_semaphore()
    partners = [(lat_o, lon), (lat, west), (lat, east), (lat_o, west), (lat_o, east), sibling]
    partners += [member((group + d) % 8) for d in range(1, 8)]
    partners += [at_y((iy + d) % 8) for d in range(1, 8)]
    partners += [at_zh((izh + d) % 4) for d in range(1, 4)]
    for p in partners:
        pl.semaphore_signal(barrier, inc=1, device_id=p, device_id_type=MESH)

    srcs = [x_hbm, cot_hbm, cells_hbm, ids_hbm, eb_hbm, spread_hbm, moves_hbm, idt_hbm,
            wqkv_hbm, wproj_hbm]
    dsts = [x_v, cot_v, cells_v, ids_v, eb_v, spread_v, moves_v, idt_v, wqkv_v, wproj_v]
    loads = [pltpu.make_async_copy(s, d, in_sem.at[i]) for i, (s, d) in enumerate(zip(srcs, dsts))]
    for cp in loads:
        cp.start()

    loads[0].wait()
    loads[1].wait()
    loads[2].wait()
    loads[3].wait()
    xc[0:TOK, 0:192] = x_v[...]
    xc[0:TOK, 192:384] = cot_v[...]
    send_b[...] = mm(cells_v[0:SENT, :], xc[0:TOK, :]).astype(BF16)
    idb[0] = jnp.zeros((16, 128), F32)
    idb[0, 0:12, 0:24] = ids_v.reshape(12, 24)[...].astype(F32)

    pl.semaphore_wait(barrier, len(partners))

    def remote(src, dst, ss, rs, dev):
        return pltpu.make_async_remote_copy(
            src_ref=src, dst_ref=dst, send_sem=ss, recv_sem=rs, device_id=dev, device_id_type=MESH)

    strip_to = [(lat_o, lon), (lat_o, lon), (lat, west), (lat_o, west)]
    id_to = [(lat_o, lon), (lat, west), (lat_o, west)]
    strips = [remote(send_b.at[pl.ds(a, n)], xc.at[pl.ds(b, n)], h_ss.at[i], h_rs.at[i], strip_to[i])
              for i, (a, b, n) in enumerate(STRIPS)]
    id_blocks = [remote(idb.at[0], idb.at[i + 1], h_ss.at[4 + i], h_rs.at[4 + i], id_to[i])
                 for i in range(3)]
    halo = [id_blocks[0], strips[0], id_blocks[1], strips[2], id_blocks[2], strips[3], strips[1]]
    for cp in halo:
        cp.start()

    loads[4].wait()
    loads[5].wait()
    eb_rows = eb_v.reshape(1728, 23)
    nothing = jnp.zeros((72, 105), F32)
    packs = []
    for g in range(3):
        acc = None
        for k in range(4):
            part = eb_rows[pl.ds(2 * (4 * g + k) + band, 72, stride=24), :]
            part = roll(jnp.concatenate([part, nothing], axis=1), 32 * k)
            acc = part if acc is None else acc + part
        packs.append(acc)
    e = jnp.concatenate(packs, axis=1)
    hi = e.astype(BF16)
    rest = e - hi.astype(F32)
    mid = rest.astype(BF16)
    low = (rest - mid.astype(F32)).astype(BF16)
    full = (mm(hi, spread_v[...]) + mm(mid, spread_v[...])) + mm(low, spread_v[...])
    for x in range(12):
        fa[pl.ds(x, 72, stride=12), :] = full[:, x * 128:(x + 1) * 128]
        tail = full[:, 1536 + (x // 8) * 128:1664 + (x // 8) * 128]
        fb[pl.ds(x, 72, stride=12), :] = roll(tail, -16 * x)

    for cp in loads[6:]:
        cp.wait()
    wq, wk, wv = wqkv_v[:, 0:192], wqkv_v[:, 192:384], wqkv_v[:, 384:576]
    lane_head = lax.broadcasted_iota(jnp.int32, (WIN, WIDTH), 1) // 32
    classes = lax.broadcasted_iota(jnp.int32, (WIN, 128), 1).astype(F32)
    ones = jnp.ones((128, 128), BF16)
    scale = 32.0 ** (-0.5)

    kept = []
    for w in range(2):
        rows = slice(w * WIN, (w + 1) * WIN)
        if w == 0:
            id_blocks[0].wait_recv()
            strips[0].wait_recv()
        else:
            for cp in halo[2:]:
                cp.wait_recv()
        width, blocks = (FAR, 2) if w == 0 else (ALL, 4)
        fr = mm(moves_v[rows, 0:width], xc[0:width, :])
        xf = fr[:, 0:192]
        cot_f = fr[:, 192:384]
        cot = cot_f.astype(BF16)
        mean = jnp.sum(xf, axis=1, keepdims=True) * (1.0 / WIDTH)
        xm = xf - mean
        var = jnp.sum(xm * xm, axis=1, keepdims=True) * (1.0 / WIDTH)
        rdev = lax.rsqrt(var + 1e-05)
        xhat = xm * rdev
        normed = xhat.astype(BF16)
        qw = mm(normed, wq).astype(BF16)
        kw = mm(normed, wk).astype(BF16)
        vw = mm(normed, wv).astype(BF16)
        daw = mm_nt(cot, wproj_v[...]).astype(BF16)

        id_all = jnp.concatenate([idb[i] for i in range(blocks)], axis=0).astype(BF16)
        id_row = mm(idt_v[rows, 0:16 * blocks], id_all) * idt_v[rows, 128:256].astype(F32)
        id_cell = mm(id_row.astype(BF16), ones)
        key = id_cell + idt_v[rows, 256:384].astype(F32) * izl.astype(F32)
        onehot = jnp.where(key == classes, 1.0, 0.0).astype(BF16)
        block = (mm_nt(onehot, onehot) - 1.0) * 1e30

        att = dq = dk = dv = None
        for h in range(HEADS):
            here = lane_head == h
            zero = jnp.zeros((WIN, WIDTH), BF16)
            qh = jnp.where(here, qw, zero)
            kh = jnp.where(here, kw, zero)
            vh = jnp.where(here, vw, zero)
            dah = jnp.where(here, daw, zero)
            hr = slice(h * WIN, (h + 1) * WIN)
            bias = jnp.concatenate([fa[hr, :], fb[hr, 0:16]], axis=1)
            s = mm_nt(qh, kw) * scale + bias + block
            ex = jnp.exp(s - jnp.max(s, axis=1, keepdims=True))
            p = ex * (1.0 / jnp.sum(ex, axis=1, keepdims=True))
            pb = p.astype(BF16)
            dp = mm_nt(dah, vw)
            ds = p * (dp - jnp.sum(p * dp, axis=1, keepdims=True))
            dsb = ds.astype(BF16)
            ds_a = ds[:, 0:128]
            ds_b = jnp.concatenate([ds[:, 128:144], jnp.zeros((WIN, 112), F32)], axis=1)
            if w == 0:
                ba[hr, :] = ds_a
                bb[hr, :] = ds_b
            else:
                ba[hr, :] += ds_a
                bb[hr, :] += ds_b
            terms = (mm(pb, vh), mm(dsb, kh), mm_tn(dsb, qh), mm_tn(pb, dah))
            if h == 0:
                att, dq, dk, dv = terms
            else:
                att, dq, dk, dv = att + terms[0], dq + terms[1], dk + terms[2], dv + terms[3]
        kept.append((normed, cot, att.astype(BF16), (dq * scale).astype(BF16),
                     (dk * scale).astype(BF16), dv.astype(BF16), cot_f, xhat, rdev))
    normed, cot, att, dq, dk, dv, cot_f, xhat, rdev = [
        jnp.concatenate(pair, axis=0) for pair in zip(*kept)]

    gs[:, 0:192] = mm_tn(normed, dq)
    gs[:, 192:384] = mm_tn(normed, dk)
    gs[:, 384:576] = mm_tn(normed, dv)
    gs[:, 576:768] = mm_tn(att, cot)
    for i in range(ROWS_MAIN):
        for j in range(COLS_MAIN):
            pay_m[main_place(i * COLS_MAIN + j)] = gs[
                i * 16:(i + 1) * 16, j * 128:(j + 1) * 128].astype(BF16)
    for half in range(2):
        for t in range(HALF, CHUNKS * MAIN):
            pay_m[half, t // MAIN, t % MAIN] = jnp.zeros((16, 128), BF16)
    cores = [remote(pay_m.at[1 - core], rc_m, c_ss.at[0], c_rs.at[0], sibling)]
    cores[0].start()

    mains, tails = [], [None, None]
    for x in range(12):
        mains.append(ba[pl.ds(x, 72, stride=12), :])
        t = roll(bb[pl.ds(x, 72, stride=12), :], 16 * x)
        tails[x // 8] = t if tails[x // 8] is None else tails[x // 8] + t
    terms = jnp.concatenate(mains + tails, axis=1)
    t_hi = terms.astype(BF16)
    t_lo = (terms - t_hi.astype(F32)).astype(BF16)
    gb = mm_nt(t_hi, spread_v[...]) + mm_nt(t_lo, spread_v[...])
    gb = jnp.concatenate([gb, jnp.zeros((8, 384), F32)], axis=0)
    for which in range(2):
        mine = jnp.where(band == which, gb, 0.0).astype(BF16)
        for t in range(BIAS_TILES):
            i, j = t // 3, t % 3
            pay_b[which, t // BIAS, t % BIAS] = mine[i * 16:(i + 1) * 16, j * 128:(j + 1) * 128]
        pay_b[which, CHUNKS - 1, BIAS - 1] = jnp.zeros((16, 128), BF16)
    cores.append(remote(pay_b.at[1 - core], rc_b, c_ss.at[1], c_rs.at[1], sibling))
    cores[1].start()

    for cp in cores:
        cp.wait_recv()
    order = [(group + d) % 8 for d in range(1, 8)]
    scatter = []
    for d, j in enumerate(order + [group]):
        cur[j, 0:MAIN] = (pay_m[core, j].astype(F32) + rc_m[j].astype(F32)).astype(BF16)
        cur[j, MAIN:TILES] = (pay_b[core, j].astype(F32) + rc_b[j].astype(F32)).astype(BF16)
        if d < 7:
            cp = remote(cur.at[j], ra.at[group], a_ss.at[d], a_rs.at[d], member(j))
            cp.start()
            scatter.append(cp)
    ra[group] = cur[group]

    dn = mm_nt(dq, wq) + mm_nt(dk, wk) + mm_nt(dv, wv)
    m1 = jnp.sum(dn, axis=1, keepdims=True) * (1.0 / WIDTH)
    m2 = jnp.sum(dn * xhat, axis=1, keepdims=True) * (1.0 / WIDTH)
    gf = (cot_f + rdev * (dn - m1 - xhat * m2)).astype(BF16)
    gback[0:TOK, :] = gf
    ret_b[...] = mm(cells_v[SENT:2 * SENT, :], gf).astype(BF16)
    ret_to = [(lat_o, lon), (lat_o, lon), (lat, east), (lat_o, east)]
    returns = [remote(ret_b.at[pl.ds(a, n)], gback.at[pl.ds(b, n)], r_ss.at[i], r_rs.at[i], ret_to[i])
               for i, (a, b, n) in enumerate(STRIPS)]
    for cp in returns:
        cp.start()

    def total(ref, n):
        acc = ref[0].astype(F32)
        for i in range(1, n):
            acc = acc + ref[i].astype(F32)
        return acc.astype(BF16)

    for cp in scatter:
        cp.wait_recv()
    ry[iy] = total(ra, 8)
    over_y = [remote(ry.at[iy], ry.at[iy], y_ss.at[d - 1], y_rs.at[d - 1], at_y((iy + d) % 8))
              for d in range(1, 8)]
    for cp in over_y:
        cp.start()

    for cp in returns:
        cp.wait_recv()
    field_ref[...] = mm(moves_v[TOK:2 * TOK, :], gback[...]).astype(BF16)

    for cp in over_y:
        cp.wait_recv()
    rz[izh] = total(ry, 8)
    over_z = [remote(rz.at[izh], rz.at[izh], z_ss.at[d - 1], z_rs.at[d - 1], at_zh((izh + d) % 4))
              for d in range(1, 4)]
    for cp in over_z:
        cp.start()
    for cp in over_z:
        cp.wait_recv()

    fin[core, group] = total(rz, 4)
    gather = [remote(fin.at[core, group], fin.at[core, group], g_ss.at[d - 1], g_rs.at[d - 1],
                     member((group + d) % 8)) for d in range(1, 8)]
    for cp in gather:
        cp.start()
    final = []
    for d in range(8):
        j = (group + 8 - d) % 8
        if d:
            gather[d - 1].wait_recv()
        cp = remote(fin.at[core, j], fin.at[core, j], k_ss.at[d], k_rs.at[d], sibling)
        cp.start()
        final.append(cp)
    for cp in final:
        cp.wait_recv()
    for cp in halo + returns + cores + scatter + over_y + over_z + gather + final:
        cp.wait_send()


def unpack(field_in, fin, field_ref, gqkv_ref, gproj_ref, gbias_ref):
    field_ref[...] = field_in[...]
    token_scale = 147456.0 ** (-0.5)
    for i in range(ROWS_MAIN):
        r = slice(i * 16, (i + 1) * 16)
        row = [fin[main_place(i * COLS_MAIN + j)].astype(F32) * token_scale for j in range(COLS_MAIN)]
        for j in range(4):
            gqkv_ref[r, j * 128:(j + 1) * 128] = row[j]
        gqkv_ref[r, 512:576] = row[4][:, 0:64]
        gproj_ref[r, 0:64] = row[4][:, 64:128]
        gproj_ref[r, 64:192] = row[5]
    bias_rows = gbias_ref.reshape(1728, 23)
    for which in range(2):
        for j in range(3):
            places = [i * 3 + j for i in range(5)]
            col = jnp.concatenate(
                [fin[which, t // BIAS, MAIN + t % BIAS] for t in places], axis=0).astype(F32)[0:72]
            for k in range(4):
                bias_rows[pl.ds(2 * (4 * j + k) + which, 72, stride=24), :] = roll(col, -32 * k)[:, 0:23]


def body(grid_state, cotangent, mask_ids, earth_bias, qkv_weight, proj_weight):
    tables = [jnp.asarray(t) for t in build_tables()]
    vm = pltpu.VMEM
    dma = lambda n: pltpu.SemaphoreType.DMA((n,))
    tiles = lambda *n: vm((*n, 16, 128), BF16)
    scratch = [
        vm((TOK, WIDTH), BF16), vm((TOK, WIDTH), BF16), vm((6, 2, 24), jnp.int32),
        vm((864, 2, 23), F32), vm((192, 576), BF16), vm((192, 192), BF16),
        vm((2 * SENT, TOK), BF16), vm((2 * TOK, ALL), BF16), vm((TOK, 384), BF16),
        vm((384, 1792), BF16),
        vm((ALL, 384), BF16), vm((SENT, 384), BF16), vm((4, 16, 128), F32),
        vm((864, 128), F32), vm((864, 128), F32), vm((864, 128), F32), vm((864, 128), F32),
        vm((ALL, WIDTH), BF16), vm((SENT, WIDTH), BF16), vm((192, 768), F32),
        tiles(2, CHUNKS, MAIN), tiles(2, CHUNKS, BIAS), tiles(CHUNKS, MAIN), tiles(CHUNKS, BIAS),
        tiles(CHUNKS, TILES), tiles(8, TILES), tiles(8, TILES), tiles(4, TILES),
        dma(10), dma(7), dma(7), dma(4), dma(4), dma(2), dma(2), dma(7), dma(7), dma(7), dma(7),
        dma(3), dma(3), dma(7), dma(7), dma(8), dma(8),
    ]
    any_space = pl.BlockSpec(memory_space=pl.ANY)
    in_vmem = pl.BlockSpec(memory_space=pltpu.VMEM)
    field, fin = pl.pallas_call(
        kernel,
        out_shape=(
            jax.ShapeDtypeStruct((TOK, WIDTH), BF16),
            jax.ShapeDtypeStruct((2, CHUNKS, TILES, 16, 128), BF16),
        ),
        in_specs=[any_space] * 10,
        out_specs=(in_vmem,) * 2,
        scratch_shapes=scratch,
        compiler_params=pltpu.CompilerParams(
            collective_id=0, has_side_effects=True, vmem_limit_bytes=48 * 2**20),
        name="window_backward",
    )(
        *[pltpu.with_memory_space_constraint(o, pltpu.HBM) for o in (grid_state.reshape(TOK, WIDTH), cotangent.reshape(TOK, WIDTH),
        mask_ids.transpose(1, 0, 2), earth_bias.transpose(1, 2, 3, 0, 4).reshape(864, 2, 23),
        qkv_weight, proj_weight, *tables)]
    )
    field, gqkv, gproj, gbias = pl.pallas_call(
        unpack,
        out_shape=(
            jax.ShapeDtypeStruct((TOK, WIDTH), BF16),
            jax.ShapeDtypeStruct((192, 576), F32),
            jax.ShapeDtypeStruct((192, 192), F32),
            jax.ShapeDtypeStruct((864, 2, 23), F32),
        ),
        in_specs=[in_vmem] * 2,
        out_specs=(in_vmem,) * 4,
        compiler_params=pltpu.CompilerParams(vmem_limit_bytes=16 * 2**20),
        name="unpack",
    )(field, fin)
    gbias = gbias.reshape(6, 12, 12, 2, 23).transpose(3, 0, 1, 2, 4)
    return field.reshape(grid_state.shape), gqkv, gproj, gbias


def solution(mesh):
    placed = (
        P(None, "lat", "lon", None),
        P(None, "lat", "lon", None),
        P(None, "lat", "lon"),
        P(),
        P(),
        P(),
    )
    return jax.shard_map(
        body,
        mesh=mesh,
        in_specs=placed,
        out_specs=(P(None, "lat", "lon", None), P(), P(), P()),
        check_vma=False,
    )
```

```python
import functools

import jax
import jax.numpy as jnp
import numpy as np
from jax import lax
from jax.experimental import pallas as pl
from jax.experimental.pallas import tpu as pltpu
from jax.sharding import PartitionSpec as P

MESH = pl.DeviceIdType.MESH
F32, BF16 = jnp.float32, jnp.bfloat16

TOK = 288
WIN = 144
WIDTH = 192
HEADS = 6
NEAR, FAR, EAST, CORNER, ALL = 288, 368, 416, 464, 512
STRIPS = ((0, NEAR, 80), (80, FAR, 48), (128, EAST, 48), (176, CORNER, 48))
SENT = 224
CHUNKS, TILES = 8, 7
MAIN, BIAS = 5, 2
HALF = 36
ROWS_MAIN, COLS_MAIN = 12, 6
BIAS_TILES = 15


def build_tables():
    natural = lambda z, r, c: (z * 6 + r) * 24 + c
    send = np.zeros((SENT, TOK), np.float32)
    for z in range(2):
        for r in range(3):
            row = z * 3 + r
            for c in range(12):
                send[row * 12 + c, natural(z, r, c + 6)] = 1
            for c in range(6):
                send[80 + row * 6 + c, natural(z, r, c + 18)] = 1
                send[128 + row * 6 + c, natural(z, r + 3, c)] = 1
                send[176 + row * 6 + c, natural(z, r, c)] = 1
    frame = np.zeros((TOK, ALL), np.float32)
    id_rows = np.zeros((TOK, 64), np.float32)
    id_cols = np.zeros((TOK, 128), np.float32)
    wrapped = np.zeros((TOK, 128), np.float32)
    for w in range(2):
        for z in range(2):
            for r in range(6):
                for p in range(12):
                    t = w * WIN + (z * 6 + r) * 12 + p
                    c = w * 12 + p
                    above = z * 3 + r - 3
                    if r < 3 and c < 18:
                        src, block, row, col = natural(z, r + 3, c + 6), 0, r + 3, c + 6
                    elif r < 3:
                        src, block, row, col = EAST + (z * 3 + r) * 6 + c - 18, 2, r + 3, c - 18
                    elif c < 12:
                        src, block, row, col = NEAR + above * 12 + c, 1, r - 3, c + 6
                    elif c < 18:
                        src, block, row, col = FAR + above * 6 + c - 12, 1, r - 3, c + 6
                    else:
                        src, block, row, col = CORNER + above * 6 + c - 18, 3, r - 3, c - 18
                    frame[t, src] = 1
                    id_rows[t, block * 16 + row * 2 + z] = 1
                    id_cols[t, col] = 1
                    wrapped[t, :] = 3.0 if r >= 3 else 0.0
    back = frame[:, TOK:].T
    out = np.concatenate([frame[:, :TOK].T, send.T], axis=1)
    spread = np.zeros((384, 1792), np.float32)
    for x in range(12):
        for b in range(12):
            for y in range(12):
                key = b * 12 + y
                col = x * 128 + key if key < 128 else 1536 + x * 16 + key - 128
                spread[b * 32 + x - y + 11, col] = 1
    cells = np.concatenate([send, back], axis=0)
    moves = np.concatenate([frame, out], axis=0)
    ids = np.concatenate([id_rows, np.zeros((TOK, 64), np.float32), id_cols, wrapped], axis=1)
    return [np.asarray(t, jnp.bfloat16) for t in (cells, moves, ids, spread)]


def mm(a, b):
    return lax.dot_general(a, b, (((1,), (0,)), ((), ())), preferred_element_type=F32)


def mm_nt(a, b):
    return lax.dot_general(a, b, (((1,), (1,)), ((), ())), preferred_element_type=F32)


def mm_tn(a, b):
    return lax.dot_general(a, b, (((0,), (0,)), ((), ())), preferred_element_type=F32)


def main_place(t):
    return t // HALF, (t % HALF) // MAIN, (t % HALF) % MAIN


def roll(a, shift):
    shift %= 128
    return pltpu.roll(a, shift, 1) if shift else a


def kernel(
    x_hbm, cot_hbm, ids_hbm, eb_hbm, wqkv_hbm, wproj_hbm, cells_hbm, moves_hbm, idt_hbm, spread_hbm,
    field_ref, fin,
    x_v, cot_v, ids_v, eb_v, wqkv_v, wproj_v, cells_v, moves_v, idt_v, spread_v,
    xc, send_b, idb, fa, fb, ba, bb, gback, ret_b, gs,
    pay_m, pay_b, rc_m, rc_b, cur, ra, ry, rz,
    in_sem, h_ss, h_rs, r_ss, r_rs, c_ss, c_rs, a_ss, a_rs, y_ss, y_rs, z_ss, z_rs,
    g_ss, g_rs, k_ss, k_rs,
):
    lat, lon = lax.axis_index("lat"), lax.axis_index("lon")
    iy, ix, izl = lat // 8, (lat // 2) % 4, lat % 2
    izh, core = lon // 2, lon % 2
    iz = izh * 2 + izl
    band = izl

    lat_o = lat + 1 - 2 * izl
    east, west = (lon + 1) % 8, (lon + 7) % 8
    sibling = (lat, izh * 2 + 1 - core)

    def pick(a, b):
        return a * (1 - core) + b * core

    def member(g):
        return (pick(iy * 8 + g, g * 8 + ix * 2 + izl), lon)

    def second(i):
        return (pick(i * 8 + ix * 2 + izl, iy * 8 + ix * 2 + i % 2), pick(lon, (i // 2) * 2 + core))

    def third(i):
        return (pick(lat, iy * 8 + i * 2 + izl), pick(i * 2 + core, lon))

    group, place2, place3 = pick(ix * 2 + izl, iy), pick(iy, iz), pick(izh, ix)
    far8, far4 = (4, 3, 5, 2, 6, 1, 7), (2, 1, 3)
    turns = ((2, 1), (1, 1), (3, 1), (2, 0), (1, 0), (3, 0), (0, 1))

    def first_to(i, way):
        dx, dz = turns[i]
        to_x, to_z = (ix + way * dx + 4) % 4, (izl + dz) % 2
        return pick(to_x * 2 + to_z, (iy + way * far8[i] + 8) % 8)

    to_first = [first_to(i, 1) for i in range(7)]
    from_first = [first_to(i, -1) for i in range(7)]
    to_second = [(place2 + d) % 8 for d in far8]
    to_third = [(place3 + d) % 4 for d in far4]

    barrier = pltpu.get_barrier_semaphore()
    partners = [(lat_o, lon), (lat, west), (lat, east), (lat_o, west), (lat_o, east), sibling]
    partners += [member(j) for j in to_first]
    partners += [second(j) for j in to_second]
    partners += [third(j) for j in to_third]
    for p in partners:
        pl.semaphore_signal(barrier, inc=1, device_id=p, device_id_type=MESH)

    srcs = [x_hbm, cot_hbm, cells_hbm, ids_hbm, eb_hbm, spread_hbm, moves_hbm, idt_hbm,
            wqkv_hbm, wproj_hbm]
    dsts = [x_v, cot_v, cells_v, ids_v, eb_v, spread_v, moves_v, idt_v, wqkv_v, wproj_v]
    loads = [pltpu.make_async_copy(s, d, in_sem.at[i]) for i, (s, d) in enumerate(zip(srcs, dsts))]
    for cp in loads:
        cp.start()

    loads[0].wait()
    loads[1].wait()
    loads[2].wait()
    loads[3].wait()
    xc[0:TOK, 0:192] = x_v[...]
    xc[0:TOK, 192:384] = cot_v[...]
    send_b[...] = mm(cells_v[0:SENT, :], xc[0:TOK, :]).astype(BF16)
    idb[0] = jnp.zeros((16, 128), F32)
    idb[0, 0:12, 0:24] = ids_v.reshape(12, 24)[...].astype(F32)

    pl.semaphore_wait(barrier, len(partners))

    def remote(src, dst, ss, rs, dev):
        return pltpu.make_async_remote_copy(
            src_ref=src, dst_ref=dst, send_sem=ss, recv_sem=rs, device_id=dev, device_id_type=MESH)

    strip_to = [(lat_o, lon), (lat_o, lon), (lat, west), (lat_o, west)]
    id_to = [(lat_o, lon), (lat, west), (lat_o, west)]
    strips = [remote(send_b.at[pl.ds(a, n)], xc.at[pl.ds(b, n)], h_ss.at[i], h_rs.at[i], strip_to[i])
              for i, (a, b, n) in enumerate(STRIPS)]
    id_blocks = [remote(idb.at[0], idb.at[i + 1], h_ss.at[4 + i], h_rs.at[4 + i], id_to[i])
                 for i in range(3)]
    halo = [id_blocks[0], strips[0], id_blocks[1], strips[2], id_blocks[2], strips[3], strips[1]]
    for cp in halo:
        cp.start()

    loads[4].wait()
    loads[5].wait()
    eb_rows = eb_v.reshape(1728, 23)
    nothing = jnp.zeros((72, 105), F32)
    packs = []
    for g in range(3):
        acc = None
        for k in range(4):
            part = eb_rows[pl.ds(2 * (4 * g + k) + band, 72, stride=24), :]
            part = roll(jnp.concatenate([part, nothing], axis=1), 32 * k)
            acc = part if acc is None else acc + part
        packs.append(acc)
    e = jnp.concatenate(packs, axis=1)
    hi = e.astype(BF16)
    rest = e - hi.astype(F32)
    mid = rest.astype(BF16)
    low = (rest - mid.astype(F32)).astype(BF16)
    full = (mm(hi, spread_v[...]) + mm(mid, spread_v[...])) + mm(low, spread_v[...])
    for x in range(12):
        fa[pl.ds(x, 72, stride=12), :] = full[:, x * 128:(x + 1) * 128]
        tail = full[:, 1536 + (x // 8) * 128:1664 + (x // 8) * 128]
        fb[pl.ds(x, 72, stride=12), :] = roll(tail, -16 * x)

    for cp in loads[6:]:
        cp.wait()
    wq, wk, wv = wqkv_v[:, 0:192], wqkv_v[:, 192:384], wqkv_v[:, 384:576]
    lane_head = lax.broadcasted_iota(jnp.int32, (WIN, WIDTH), 1) // 32
    classes = lax.broadcasted_iota(jnp.int32, (WIN, 128), 1).astype(F32)
    ones = jnp.ones((128, 128), BF16)
    scale = 32.0 ** (-0.5)

    kept = []
    for w in range(2):
        rows = slice(w * WIN, (w + 1) * WIN)
        if w == 0:
            id_blocks[0].wait_recv()
            strips[0].wait_recv()
        else:
            for cp in halo[2:]:
                cp.wait_recv()
        width, blocks = (FAR, 2) if w == 0 else (ALL, 4)
        fr = mm(moves_v[rows, 0:width], xc[0:width, :])
        xf = fr[:, 0:192]
        cot_f = fr[:, 192:384]
        cot = cot_f.astype(BF16)
        mean = jnp.sum(xf, axis=1, keepdims=True) * (1.0 / WIDTH)
        xm = xf - mean
        var = jnp.sum(xm * xm, axis=1, keepdims=True) * (1.0 / WIDTH)
        rdev = lax.rsqrt(var + 1e-05)
        xhat = xm * rdev
        normed = xhat.astype(BF16)
        qw = mm(normed, wq).astype(BF16)
        kw = mm(normed, wk).astype(BF16)
        vw = mm(normed, wv).astype(BF16)
        daw = mm_nt(cot, wproj_v[...]).astype(BF16)

        id_all = jnp.concatenate([idb[i] for i in range(blocks)], axis=0).astype(BF16)
        id_row = mm(idt_v[rows, 0:16 * blocks], id_all) * idt_v[rows, 128:256].astype(F32)
        id_cell = mm(id_row.astype(BF16), ones)
        key = id_cell + idt_v[rows, 256:384].astype(F32) * izl.astype(F32)
        onehot = jnp.where(key == classes, 1.0, 0.0).astype(BF16)
        block = (mm_nt(onehot, onehot) - 1.0) * 1e30

        att = dq = dk = dv = None
        for h in range(HEADS):
            here = lane_head == h
            zero = jnp.zeros((WIN, WIDTH), BF16)
            qh = jnp.where(here, qw, zero)
            kh = jnp.where(here, kw, zero)
            vh = jnp.where(here, vw, zero)
            dah = jnp.where(here, daw, zero)
            hr = slice(h * WIN, (h + 1) * WIN)
            bias = jnp.concatenate([fa[hr, :], fb[hr, 0:16]], axis=1)
            s = mm_nt(qh, kw) * scale + bias + block
            ex = jnp.exp(s - jnp.max(s, axis=1, keepdims=True))
            p = ex * (1.0 / jnp.sum(ex, axis=1, keepdims=True))
            pb = p.astype(BF16)
            dp = mm_nt(dah, vw)
            ds = p * (dp - jnp.sum(p * dp, axis=1, keepdims=True))
            dsb = ds.astype(BF16)
            ds_a = ds[:, 0:128]
            ds_b = jnp.concatenate([ds[:, 128:144], jnp.zeros((WIN, 112), F32)], axis=1)
            if w == 0:
                ba[hr, :] = ds_a
                bb[hr, :] = ds_b
            else:
                ba[hr, :] += ds_a
                bb[hr, :] += ds_b
            terms = (mm(pb, vh), mm(dsb, kh), mm_tn(dsb, qh), mm_tn(pb, dah))
            if h == 0:
                att, dq, dk, dv = terms
            else:
                att, dq, dk, dv = att + terms[0], dq + terms[1], dk + terms[2], dv + terms[3]
        kept.append((normed, cot, att.astype(BF16), (dq * scale).astype(BF16),
                     (dk * scale).astype(BF16), dv.astype(BF16), cot_f, xhat, rdev))
    normed, cot, att, dq, dk, dv, cot_f, xhat, rdev = [
        jnp.concatenate(pair, axis=0) for pair in zip(*kept)]

    gs[:, 0:192] = mm_tn(normed, dq)
    gs[:, 192:384] = mm_tn(normed, dk)
    gs[:, 384:576] = mm_tn(normed, dv)
    gs[:, 576:768] = mm_tn(att, cot)
    for i in range(ROWS_MAIN):
        for j in range(COLS_MAIN):
            pay_m[main_place(i * COLS_MAIN + j)] = gs[
                i * 16:(i + 1) * 16, j * 128:(j + 1) * 128].astype(BF16)
    for half in range(2):
        for t in range(HALF, CHUNKS * MAIN):
            pay_m[half, t // MAIN, t % MAIN] = jnp.zeros((16, 128), BF16)
    cores = [remote(pay_m.at[1 - core], rc_m, c_ss.at[0], c_rs.at[0], sibling)]
    cores[0].start()

    mains, tails = [], [None, None]
    for x in range(12):
        mains.append(ba[pl.ds(x, 72, stride=12), :])
        t = roll(bb[pl.ds(x, 72, stride=12), :], 16 * x)
        tails[x // 8] = t if tails[x // 8] is None else tails[x // 8] + t
    terms = jnp.concatenate(mains + tails, axis=1)
    t_hi = terms.astype(BF16)
    t_lo = (terms - t_hi.astype(F32)).astype(BF16)
    gb = mm_nt(t_hi, spread_v[...]) + mm_nt(t_lo, spread_v[...])
    gb = jnp.concatenate([gb, jnp.zeros((8, 384), F32)], axis=0)
    for which in range(2):
        mine = jnp.where(band == which, gb, 0.0).astype(BF16)
        for t in range(BIAS_TILES):
            i, j = t // 3, t % 3
            pay_b[which, t // BIAS, t % BIAS] = mine[i * 16:(i + 1) * 16, j * 128:(j + 1) * 128]
        pay_b[which, CHUNKS - 1, BIAS - 1] = jnp.zeros((16, 128), BF16)
    cores.append(remote(pay_b.at[1 - core], rc_b, c_ss.at[1], c_rs.at[1], sibling))
    cores[1].start()

    for cp in cores:
        cp.wait_recv()
    scatter = []
    for d, j in enumerate(to_first + [group]):
        cur[j, 0:MAIN] = (pay_m[core, j].astype(F32) + rc_m[j].astype(F32)).astype(BF16)
        cur[j, MAIN:TILES] = (pay_b[core, j].astype(F32) + rc_b[j].astype(F32)).astype(BF16)
        if d < 7:
            cp = remote(cur.at[j], ra.at[group], a_ss.at[d], a_rs.at[d], member(j))
            cp.start()
            scatter.append(cp)
    ra[group] = cur[group]

    dn = mm_nt(dq, wq) + mm_nt(dk, wk) + mm_nt(dv, wv)
    m1 = jnp.sum(dn, axis=1, keepdims=True) * (1.0 / WIDTH)
    m2 = jnp.sum(dn * xhat, axis=1, keepdims=True) * (1.0 / WIDTH)
    gf = (cot_f + rdev * (dn - m1 - xhat * m2)).astype(BF16)
    gback[0:TOK, :] = gf
    ret_b[...] = mm(cells_v[SENT:2 * SENT, :], gf).astype(BF16)
    ret_to = [(lat_o, lon), (lat_o, lon), (lat, east), (lat_o, east)]
    returns = [remote(ret_b.at[pl.ds(a, n)], gback.at[pl.ds(b, n)], r_ss.at[i], r_rs.at[i], ret_to[i])
               for i, (a, b, n) in enumerate(STRIPS)]
    for cp in returns:
        cp.start()

    def total(ref, n):
        acc = ref[0].astype(F32)
        for i in range(1, n):
            acc = acc + ref[i].astype(F32)
        return acc.astype(BF16)

    for cp in scatter:
        cp.wait_recv()
    ry[place2] = total(ra, 8)
    over_y = [remote(ry.at[place2], ry.at[place2], y_ss.at[i], y_rs.at[i], second(j))
              for i, j in enumerate(to_second)]
    for cp in over_y:
        cp.start()

    for cp in returns:
        cp.wait_recv()
    field_ref[...] = mm(moves_v[TOK:2 * TOK, :], gback[...]).astype(BF16)

    for cp in over_y:
        cp.wait_recv()
    rz[place3] = total(ry, 8)
    over_z = [remote(rz.at[place3], rz.at[place3], z_ss.at[i], z_rs.at[i], third(j))
              for i, j in enumerate(to_third)]
    for cp in over_z:
        cp.start()
    for cp in over_z:
        cp.wait_recv()

    fin[core, group] = total(rz, 4)
    gather = [remote(fin.at[core, group], fin.at[core, group], g_ss.at[i], g_rs.at[i], member(j))
              for i, j in enumerate(to_first)]
    for cp in gather:
        cp.start()
    final = []
    for i in (7, 6, 5, 4, 3, 2, 1, 0):
        if i < 7:
            gather[i].wait_recv()
        j = group if i == 7 else from_first[i]
        cp = remote(fin.at[core, j], fin.at[core, j], k_ss.at[i], k_rs.at[i], sibling)
        cp.start()
        final.append(cp)
    for cp in final:
        cp.wait_recv()
    for cp in halo + returns + cores + scatter + over_y + over_z + gather + final:
        cp.wait_send()


def unpack(field_in, fin, field_ref, gqkv_ref, gproj_ref, gbias_ref):
    field_ref[...] = field_in[...]
    token_scale = 147456.0 ** (-0.5)
    for i in range(ROWS_MAIN):
        r = slice(i * 16, (i + 1) * 16)
        row = [fin[main_place(i * COLS_MAIN + j)].astype(F32) * token_scale for j in range(COLS_MAIN)]
        for j in range(4):
            gqkv_ref[r, j * 128:(j + 1) * 128] = row[j]
        gqkv_ref[r, 512:576] = row[4][:, 0:64]
        gproj_ref[r, 0:64] = row[4][:, 64:128]
        gproj_ref[r, 64:192] = row[5]
    bias_rows = gbias_ref.reshape(1728, 23)
    for which in range(2):
        for j in range(3):
            places = [i * 3 + j for i in range(5)]
            col = jnp.concatenate(
                [fin[which, t // BIAS, MAIN + t % BIAS] for t in places], axis=0).astype(F32)[0:72]
            for k in range(4):
                bias_rows[pl.ds(2 * (4 * j + k) + which, 72, stride=24), :] = roll(col, -32 * k)[:, 0:23]


def body(grid_state, cotangent, mask_ids, earth_bias, qkv_weight, proj_weight):
    tables = [jnp.asarray(t) for t in build_tables()]
    vm = pltpu.VMEM
    dma = lambda n: pltpu.SemaphoreType.DMA((n,))
    tiles = lambda *n: vm((*n, 16, 128), BF16)
    scratch = [
        vm((TOK, WIDTH), BF16), vm((TOK, WIDTH), BF16), vm((6, 2, 24), jnp.int32),
        vm((864, 2, 23), F32), vm((192, 576), BF16), vm((192, 192), BF16),
        vm((2 * SENT, TOK), BF16), vm((2 * TOK, ALL), BF16), vm((TOK, 384), BF16),
        vm((384, 1792), BF16),
        vm((ALL, 384), BF16), vm((SENT, 384), BF16), vm((4, 16, 128), F32),
        vm((864, 128), F32), vm((864, 128), F32), vm((864, 128), F32), vm((864, 128), F32),
        vm((ALL, WIDTH), BF16), vm((SENT, WIDTH), BF16), vm((192, 768), F32),
        tiles(2, CHUNKS, MAIN), tiles(2, CHUNKS, BIAS), tiles(CHUNKS, MAIN), tiles(CHUNKS, BIAS),
        tiles(CHUNKS, TILES), tiles(8, TILES), tiles(8, TILES), tiles(4, TILES),
        dma(10), dma(7), dma(7), dma(4), dma(4), dma(2), dma(2), dma(7), dma(7), dma(7), dma(7),
        dma(3), dma(3), dma(7), dma(7), dma(8), dma(8),
    ]
    any_space = pl.BlockSpec(memory_space=pl.ANY)
    in_vmem = pl.BlockSpec(memory_space=pltpu.VMEM)
    field, fin = pl.pallas_call(
        kernel,
        out_shape=(
            jax.ShapeDtypeStruct((TOK, WIDTH), BF16),
            jax.ShapeDtypeStruct((2, CHUNKS, TILES, 16, 128), BF16),
        ),
        in_specs=[any_space] * 10,
        out_specs=(in_vmem,) * 2,
        scratch_shapes=scratch,
        compiler_params=pltpu.CompilerParams(
            collective_id=0, has_side_effects=True, vmem_limit_bytes=48 * 2**20),
        name="window_backward",
    )(
        *[pltpu.with_memory_space_constraint(o, pltpu.HBM) for o in (grid_state.reshape(TOK, WIDTH), cotangent.reshape(TOK, WIDTH),
        mask_ids.transpose(1, 0, 2), earth_bias.transpose(1, 2, 3, 0, 4).reshape(864, 2, 23),
        qkv_weight, proj_weight, *tables)]
    )
    field, gqkv, gproj, gbias = pl.pallas_call(
        unpack,
        out_shape=(
            jax.ShapeDtypeStruct((TOK, WIDTH), BF16),
            jax.ShapeDtypeStruct((192, 576), F32),
            jax.ShapeDtypeStruct((192, 192), F32),
            jax.ShapeDtypeStruct((864, 2, 23), F32),
        ),
        in_specs=[in_vmem] * 2,
        out_specs=(in_vmem,) * 4,
        compiler_params=pltpu.CompilerParams(vmem_limit_bytes=16 * 2**20),
        name="unpack",
    )(field, fin)
    gbias = gbias.reshape(6, 12, 12, 2, 23).transpose(3, 0, 1, 2, 4)
    return field.reshape(grid_state.shape), gqkv, gproj, gbias


def solution(mesh):
    placed = (
        P(None, "lat", "lon", None),
        P(None, "lat", "lon", None),
        P(None, "lat", "lon"),
        P(),
        P(),
        P(),
    )
    return jax.shard_map(
        body,
        mesh=mesh,
        in_specs=placed,
        out_specs=(P(None, "lat", "lon", None), P(), P(), P()),
        check_vma=False,
    )
```

```python
import functools

import jax
import jax.numpy as jnp
import numpy as np
from jax import lax
from jax.experimental import pallas as pl
from jax.experimental.pallas import tpu as pltpu
from jax.sharding import PartitionSpec as P

MESH = pl.DeviceIdType.MESH
F32, BF16 = jnp.float32, jnp.bfloat16

TOK = 288
WIN = 144
WIDTH = 192
HEADS = 6
SWAP, EAST, CORNER, ALL = 288, 400, 448, 496
STRIPS = ((0, SWAP, 112), (112, EAST, 48), (160, CORNER, 48))
SENT = 208
STACK = 6
CHUNKS, TILES = 8, 7
MAIN, BIAS = 5, 2
HALF = 36
ROWS_MAIN, COLS_MAIN = 12, 6
BIAS_TILES = 15


def build_tables():
    natural = lambda z, r, c: (z * 6 + r) * 24 + c
    send = np.zeros((SENT, TOK), np.float32)
    for z in range(2):
        for r in range(3):
            row = z * 3 + r
            for c in range(18):
                send[row * 18 + c, natural(z, r, c + 6)] = 1
            for c in range(6):
                send[112 + row * 6 + c, natural(z, r + 3, c)] = 1
                send[160 + row * 6 + c, natural(z, r, c)] = 1
    frame = np.zeros((TOK, ALL), np.float32)
    id_rows = np.zeros((TOK, 64), np.float32)
    id_cols = np.zeros((TOK, 128), np.float32)
    wrapped = np.zeros((TOK, 128), np.float32)
    for w in range(2):
        for z in range(2):
            for r in range(6):
                for p in range(12):
                    t = w * WIN + (z * 6 + r) * 12 + p
                    c = w * 12 + p
                    above = z * 3 + r - 3
                    if r < 3 and c < 18:
                        src, block, row, col = natural(z, r + 3, c + 6), 0, r + 3, c + 6
                    elif r < 3:
                        src, block, row, col = EAST + (z * 3 + r) * 6 + c - 18, 2, r + 3, c - 18
                    elif c < 18:
                        src, block, row, col = SWAP + above * 18 + c, 1, r - 3, c + 6
                    else:
                        src, block, row, col = CORNER + above * 6 + c - 18, 3, r - 3, c - 18
                    frame[t, src] = 1
                    id_rows[t, block * 16 + row * 2 + z] = 1
                    id_cols[t, col] = 1
                    wrapped[t, :] = 3.0 if r >= 3 else 0.0
    back = frame[:, TOK:].T
    out = np.concatenate([frame[:, :TOK].T, send.T], axis=1)
    spread = np.zeros((384, 1792), np.float32)
    for x in range(12):
        for b in range(12):
            for y in range(12):
                key = b * 12 + y
                col = x * 128 + key if key < 128 else 1536 + x * 16 + key - 128
                spread[b * 32 + x - y + 11, col] = 1
    cells = np.concatenate([send, back], axis=0)
    moves = np.concatenate([frame, out], axis=0)
    ids = np.concatenate([id_rows, np.zeros((TOK, 64), np.float32), id_cols, wrapped], axis=1)
    return [np.asarray(t, jnp.bfloat16) for t in (cells, moves, ids, spread)]


def mm(a, b):
    return lax.dot_general(a, b, (((1,), (0,)), ((), ())), preferred_element_type=F32)


def mm_nt(a, b):
    return lax.dot_general(a, b, (((1,), (1,)), ((), ())), preferred_element_type=F32)


def mm_tn(a, b):
    return lax.dot_general(a, b, (((0,), (0,)), ((), ())), preferred_element_type=F32)


def main_place(t):
    return t // HALF, (t % HALF) // MAIN, (t % HALF) % MAIN


def roll(a, shift):
    shift %= 128
    return pltpu.roll(a, shift, 1) if shift else a


def kernel(
    x_hbm, cot_hbm, ids_hbm, eb_hbm, wqkv_hbm, wproj_hbm, cells_hbm, moves_hbm, idt_hbm, spread_hbm,
    field_ref, fin,
    x_v, cot_v, ids_v, eb_v, wqkv_v, wproj_v, cells_v, moves_v, idt_v, spread_v,
    xc, send_b, idb, fa, fb, ba, bb, gback, ret_b, dqkv,
    pay_m, pay_b, rc_m, rc_b, cur, ra, ry, rz,
    in_sem, h_ss, h_rs, r_ss, r_rs, c_ss, c_rs, a_ss, a_rs, y_ss, y_rs, z_ss, z_rs,
    g_ss, g_rs, k_ss, k_rs,
):
    lat, lon = lax.axis_index("lat"), lax.axis_index("lon")
    iy, ix, izl = lat // 8, (lat // 2) % 4, lat % 2
    izh, core = lon // 2, lon % 2
    iz = izh * 2 + izl
    band = izl

    lat_o = lat + 1 - 2 * izl
    east, west = (lon + 1) % 8, (lon + 7) % 8
    sibling = (lat, izh * 2 + 1 - core)

    def pick(a, b):
        return a * (1 - core) + b * core

    def member(g):
        return (pick(iy * 8 + g, g * 8 + ix * 2 + izl), lon)

    def second(i):
        return (pick(i * 8 + ix * 2 + izl, iy * 8 + ix * 2 + i % 2), pick(lon, (i // 2) * 2 + core))

    def third(i):
        return (pick(lat, iy * 8 + i * 2 + izl), pick(i * 2 + core, lon))

    group, place2, place3 = pick(ix * 2 + izl, iy), pick(iy, iz), pick(izh, ix)
    far8, far4 = (4, 3, 5, 2, 6, 1, 7), (2, 1, 3)
    turns = ((2, 1), (1, 1), (3, 1), (2, 0), (1, 0), (3, 0), (0, 1))

    def first_to(i, way):
        dx, dz = turns[i]
        to_x, to_z = (ix + way * dx + 4) % 4, (izl + dz) % 2
        return pick(to_x * 2 + to_z, (iy + way * far8[i] + 8) % 8)

    to_first = [first_to(i, 1) for i in range(7)]
    from_first = [first_to(i, -1) for i in range(7)]
    to_second = [(place2 + d) % 8 for d in far8]
    to_third = [(place3 + d) % 4 for d in far4]

    srcs = [x_hbm, cot_hbm, cells_hbm, ids_hbm, eb_hbm, spread_hbm, moves_hbm, idt_hbm,
            wqkv_hbm, wproj_hbm]
    dsts = [x_v, cot_v, cells_v, ids_v, eb_v, spread_v, moves_v, idt_v, wqkv_v, wproj_v]
    loads = [pltpu.make_async_copy(s, d, in_sem.at[i]) for i, (s, d) in enumerate(zip(srcs, dsts))]
    for cp in loads[:4]:
        cp.start()

    barrier = pltpu.get_barrier_semaphore()
    partners = [(lat_o, lon), (lat, west), (lat, east), (lat_o, west), (lat_o, east), sibling]
    partners += [member(j) for j in to_first]
    partners += [second(j) for j in to_second]
    partners += [third(j) for j in to_third]
    for p in partners:
        pl.semaphore_signal(barrier, inc=1, device_id=p, device_id_type=MESH)
    for cp in loads[4:]:
        cp.start()

    loads[0].wait()
    loads[1].wait()
    loads[2].wait()
    loads[3].wait()
    xc[0:TOK, 0:128] = x_v[:, 0:128]
    xc[0:TOK, 128:256] = cot_v[:, 0:128]
    xc[0:TOK, 256:384] = jnp.concatenate([x_v[:, 128:192], cot_v[:, 128:192]], axis=1)
    send_b[...] = mm(cells_v[0:SENT, :], xc[0:TOK, :]).astype(BF16)
    rows_id = jnp.concatenate([ids_v.reshape(12, 24)[...].astype(F32), jnp.zeros((4, 24), F32)], axis=0)
    idb[0] = jnp.concatenate([rows_id, jnp.zeros((16, 104), F32)], axis=1).astype(BF16)

    pl.semaphore_wait(barrier, len(partners))

    def remote(src, dst, ss, rs, dev):
        return pltpu.make_async_remote_copy(
            src_ref=src, dst_ref=dst, send_sem=ss, recv_sem=rs, device_id=dev, device_id_type=MESH)

    strip_to = [(lat_o, lon), (lat, west), (lat_o, west)]
    id_to = [(lat_o, lon), (lat, west), (lat_o, west)]
    strips = [remote(send_b.at[pl.ds(a, n)], xc.at[pl.ds(b, n)], h_ss.at[i], h_rs.at[i], strip_to[i])
              for i, (a, b, n) in enumerate(STRIPS)]
    id_blocks = [remote(idb.at[0], idb.at[i + 1], h_ss.at[3 + i], h_rs.at[3 + i], id_to[i])
                 for i in range(3)]
    halo = [strips[2], strips[0], strips[1]] + id_blocks
    for cp in halo:
        cp.start()

    loads[4].wait()
    loads[5].wait()
    eb_rows = eb_v.reshape(1728, 23)
    nothing = jnp.zeros((72, 105), F32)
    packs = []
    for g in range(3):
        acc = None
        for k in range(4):
            part = eb_rows[pl.ds(2 * (4 * g + k) + band, 72, stride=24), :]
            part = roll(jnp.concatenate([part, nothing], axis=1), 32 * k)
            acc = part if acc is None else acc + part
        packs.append(acc)
    e = jnp.concatenate(packs, axis=1)
    hi = e.astype(BF16)
    rest = e - hi.astype(F32)
    mid = rest.astype(BF16)
    low = (rest - mid.astype(F32)).astype(BF16)
    full = (mm(hi, spread_v[...]) + mm(mid, spread_v[...])) + mm(low, spread_v[...])
    for x in range(12):
        fa[pl.ds(x, 72, stride=12), :] = full[:, x * 128:(x + 1) * 128]
        tail = full[:, 1536 + (x // 8) * 128:1664 + (x // 8) * 128]
        fb[pl.ds(x, 72, stride=12), :] = roll(tail, -16 * x)

    for cp in loads[6:]:
        cp.wait()
    lane_head = lax.broadcasted_iota(jnp.int32, (WIN, WIDTH), 1) // 32
    classes = lax.broadcasted_iota(jnp.int32, (TOK, 128), 1).astype(F32)
    scale = 32.0 ** (-0.5)
    for cp in halo:
        cp.wait_recv()

    fr = mm(moves_v[0:TOK, :], xc[...])
    xf = jnp.concatenate([fr[:, 0:128], fr[:, 256:320]], axis=1)
    cot_f = jnp.concatenate([fr[:, 128:256], fr[:, 320:384]], axis=1)
    cot = cot_f.astype(BF16)
    mean = jnp.sum(xf, axis=1, keepdims=True) * (1.0 / WIDTH)
    xm = xf - mean
    var = jnp.sum(xm * xm, axis=1, keepdims=True) * (1.0 / WIDTH)
    rdev = lax.rsqrt(var + 1e-05)
    xhat = xm * rdev
    normed = xhat.astype(BF16)
    q = mm(normed, wqkv_v[:, 0:192]).astype(BF16)
    k = mm(normed, wqkv_v[:, 192:384]).astype(BF16)
    v = mm(normed, wqkv_v[:, 384:576]).astype(BF16)
    da = mm_nt(cot, wproj_v[...]).astype(BF16)

    id_all = jnp.concatenate([idb[i] for i in range(4)], axis=0)
    id_row = mm(idt_v[:, 0:64], id_all) * idt_v[:, 128:256].astype(F32)
    id_cell = mm(id_row.astype(BF16), jnp.ones((128, 128), BF16))
    key = id_cell + idt_v[:, 256:384].astype(F32) * izl.astype(F32)
    onehot = jnp.where(key == classes, 1.0, 0.0).astype(BF16)

    def spread_heads(a, heads):
        zero = jnp.zeros((WIN, WIDTH), BF16)
        return jnp.concatenate([jnp.where(lane_head == h, a, zero) for h in heads], axis=0)

    def own_lanes(a, heads, acc):
        for i, h in enumerate(heads):
            part = a[i * WIN:(i + 1) * WIN]
            acc = part if acc is None else jnp.where(lane_head == h, part, acc)
        return acc

    atts = []
    for w in range(2):
        rows = slice(w * WIN, (w + 1) * WIN)
        qw, kw, vw, daw = q[rows], k[rows], v[rows], da[rows]
        block = (mm_nt(onehot[rows], onehot[rows]) - 1.0) * 1e30
        att = dq = dk = dv = None
        for h0 in range(0, HEADS, STACK):
            heads = range(h0, h0 + STACK)
            qh, dah = spread_heads(qw, heads), spread_heads(daw, heads)
            hr = slice(h0 * WIN, (h0 + STACK) * WIN)
            bias = jnp.concatenate([fa[hr, :], fb[hr, 0:16]], axis=1)
            s = mm_nt(qh, kw) * scale + bias + jnp.concatenate([block] * STACK, axis=0)
            ex = jnp.exp(s - jnp.max(s, axis=1, keepdims=True))
            p = ex * (1.0 / jnp.sum(ex, axis=1, keepdims=True))
            pb = p.astype(BF16)
            dp = mm_nt(dah, vw)
            ds = p * (dp - jnp.sum(p * dp, axis=1, keepdims=True))
            dsb = ds.astype(BF16)
            ds_a = ds[:, 0:128]
            ds_b = jnp.concatenate([ds[:, 128:144], jnp.zeros((STACK * WIN, 112), F32)], axis=1)
            if w == 0:
                ba[hr, :] = ds_a
                bb[hr, :] = ds_b
            else:
                ba[hr, :] += ds_a
                bb[hr, :] += ds_b
            att = own_lanes(mm(pb, vw), heads, att)
            dq = own_lanes(mm(dsb, kw), heads, dq)
            dk_part, dv_part = mm_tn(dsb, qh), mm_tn(pb, dah)
            dk = dk_part if dk is None else dk + dk_part
            dv = dv_part if dv is None else dv + dv_part
        atts.append(att.astype(BF16))
        dqkv[rows, 0:192] = (dq * scale).astype(BF16)
        dqkv[rows, 192:384] = (dk * scale).astype(BF16)
        dqkv[rows, 384:576] = dv.astype(BF16)
    att = jnp.concatenate(atts, axis=0)

    g_qkv = mm_tn(normed, dqkv[...])
    g_proj = mm_tn(att, cot)
    g_mix = jnp.concatenate([g_qkv[:, 512:576], g_proj[:, 128:192]], axis=1)
    columns = [g_qkv[:, j * 128:(j + 1) * 128] for j in range(4)] + [g_mix, g_proj[:, 0:128]]
    for i in range(ROWS_MAIN):
        for j in range(COLS_MAIN):
            pay_m[main_place(i * COLS_MAIN + j)] = columns[j][i * 16:(i + 1) * 16].astype(BF16)
    for half in range(2):
        for t in range(HALF, CHUNKS * MAIN):
            pay_m[half, t // MAIN, t % MAIN] = jnp.zeros((16, 128), BF16)
    cores = [remote(pay_m.at[1 - core], rc_m, c_ss.at[0], c_rs.at[0], sibling)]
    cores[0].start()

    mains, tails = [], [None, None]
    for x in range(12):
        mains.append(ba[pl.ds(x, 72, stride=12), :])
        t = roll(bb[pl.ds(x, 72, stride=12), :], 16 * x)
        tails[x // 8] = t if tails[x // 8] is None else tails[x // 8] + t
    terms = jnp.concatenate(mains + tails, axis=1)
    t_hi = terms.astype(BF16)
    t_lo = (terms - t_hi.astype(F32)).astype(BF16)
    gb = mm_nt(t_hi, spread_v[...]) + mm_nt(t_lo, spread_v[...])
    gb = jnp.concatenate([gb, jnp.zeros((8, 384), F32)], axis=0)
    for which in range(2):
        mine = jnp.where(band == which, gb, 0.0).astype(BF16)
        for t in range(BIAS_TILES):
            i, j = t // 3, t % 3
            pay_b[which, t // BIAS, t % BIAS] = mine[i * 16:(i + 1) * 16, j * 128:(j + 1) * 128]
        pay_b[which, CHUNKS - 1, BIAS - 1] = jnp.zeros((16, 128), BF16)
    cores.append(remote(pay_b.at[1 - core], rc_b, c_ss.at[1], c_rs.at[1], sibling))
    cores[1].start()

    for cp in cores:
        cp.wait_recv()
    scatter = []
    for d, j in enumerate(to_first + [group]):
        cur[j, 0:MAIN] = (pay_m[core, j].astype(F32) + rc_m[j].astype(F32)).astype(BF16)
        cur[j, MAIN:TILES] = (pay_b[core, j].astype(F32) + rc_b[j].astype(F32)).astype(BF16)
        if d < 7:
            cp = remote(cur.at[j], ra.at[group], a_ss.at[d], a_rs.at[d], member(j))
            cp.start()
            scatter.append(cp)
    ra[group] = cur[group]

    dn = mm_nt(dqkv[...], wqkv_v[...])
    m1 = jnp.sum(dn, axis=1, keepdims=True) * (1.0 / WIDTH)
    m2 = jnp.sum(dn * xhat, axis=1, keepdims=True) * (1.0 / WIDTH)
    gf = (cot_f + rdev * (dn - m1 - xhat * m2)).astype(BF16)
    gback[0:TOK, :] = gf
    ret_b[...] = mm(cells_v[SENT:2 * SENT, :], gf).astype(BF16)
    ret_to = [(lat_o, lon), (lat, east), (lat_o, east)]
    returns = [remote(ret_b.at[pl.ds(a, n)], gback.at[pl.ds(b, n)], r_ss.at[i], r_rs.at[i], ret_to[i])
               for i, (a, b, n) in enumerate(STRIPS)]
    for cp in returns:
        cp.start()

    def total(ref, n):
        acc = ref[0].astype(F32)
        for i in range(1, n):
            acc = acc + ref[i].astype(F32)
        return acc.astype(BF16)

    for cp in scatter:
        cp.wait_recv()
    ry[place2] = total(ra, 8)
    over_y = [remote(ry.at[place2], ry.at[place2], y_ss.at[i], y_rs.at[i], second(j))
              for i, j in enumerate(to_second)]
    for cp in over_y:
        cp.start()

    for cp in returns:
        cp.wait_recv()
    field_ref[...] = mm(moves_v[TOK:2 * TOK, :], gback[...]).astype(BF16)

    for cp in over_y:
        cp.wait_recv()
    rz[place3] = total(ry, 8)
    over_z = [remote(rz.at[place3], rz.at[place3], z_ss.at[i], z_rs.at[i], third(j))
              for i, j in enumerate(to_third)]
    for cp in over_z:
        cp.start()
    for cp in over_z:
        cp.wait_recv()

    fin[core, group] = total(rz, 4)
    gather = [remote(fin.at[core, group], fin.at[core, group], g_ss.at[i], g_rs.at[i], member(j))
              for i, j in enumerate(to_first)]
    for cp in gather:
        cp.start()
    final = []
    for i in (7, 6, 5, 4, 3, 2, 1, 0):
        if i < 7:
            gather[i].wait_recv()
        j = group if i == 7 else from_first[i]
        cp = remote(fin.at[core, j], fin.at[core, j], k_ss.at[i], k_rs.at[i], sibling)
        cp.start()
        final.append(cp)
    for cp in final:
        cp.wait_recv()
    for cp in halo + returns + cores + scatter + over_y + over_z + gather + final:
        cp.wait_send()


def unpack(field_in, fin, field_hbm, gqkv_hbm, gproj_hbm, gbias_hbm, gqkv_ref, gproj_ref, gbias_ref, sem):
    outs = [(field_in, field_hbm), (gqkv_ref, gqkv_hbm), (gproj_ref, gproj_hbm), (gbias_ref, gbias_hbm)]
    stores = [pltpu.make_async_copy(src, dst, sem.at[i]) for i, (src, dst) in enumerate(outs)]
    stores[0].start()
    token_scale = 147456.0 ** (-0.5)
    for i in range(ROWS_MAIN):
        r = slice(i * 16, (i + 1) * 16)
        row = [fin[main_place(i * COLS_MAIN + j)].astype(F32) * token_scale for j in range(COLS_MAIN)]
        for j in range(4):
            gqkv_ref[r, j * 128:(j + 1) * 128] = row[j]
        gqkv_ref[r, 512:576] = row[4][:, 0:64]
        gproj_ref[r, 0:128] = row[5]
        gproj_ref[r, 128:192] = row[4][:, 64:128]
    stores[1].start()
    stores[2].start()
    bias_rows = gbias_ref.reshape(1728, 23)
    for which in range(2):
        for j in range(3):
            places = [i * 3 + j for i in range(5)]
            col = jnp.concatenate(
                [fin[which, t // BIAS, MAIN + t % BIAS] for t in places], axis=0).astype(F32)[0:72]
            for k in range(4):
                bias_rows[pl.ds(2 * (4 * j + k) + which, 72, stride=24), :] = roll(col, -32 * k)[:, 0:23]
    stores[3].start()
    for cp in stores:
        cp.wait()


def body(grid_state, cotangent, mask_ids, earth_bias, qkv_weight, proj_weight):
    tables = [jnp.asarray(t) for t in build_tables()]
    vm = pltpu.VMEM
    dma = lambda n: pltpu.SemaphoreType.DMA((n,))
    tiles = lambda *n: vm((*n, 16, 128), BF16)
    scratch = [
        vm((TOK, WIDTH), BF16), vm((TOK, WIDTH), BF16), vm((6, 2, 24), jnp.int32),
        vm((864, 2, 23), F32), vm((192, 576), BF16), vm((192, 192), BF16),
        vm((2 * SENT, TOK), BF16), vm((2 * TOK, ALL), BF16), vm((TOK, 384), BF16),
        vm((384, 1792), BF16),
        vm((ALL, 384), BF16), vm((SENT, 384), BF16), vm((4, 16, 128), BF16),
        vm((864, 128), F32), vm((864, 128), F32), vm((864, 128), F32), vm((864, 128), F32),
        vm((ALL, WIDTH), BF16), vm((SENT, WIDTH), BF16), vm((TOK, 576), BF16),
        tiles(2, CHUNKS, MAIN), tiles(2, CHUNKS, BIAS), tiles(CHUNKS, MAIN), tiles(CHUNKS, BIAS),
        tiles(CHUNKS, TILES), tiles(8, TILES), tiles(8, TILES), tiles(4, TILES),
        dma(10), dma(6), dma(6), dma(3), dma(3), dma(2), dma(2), dma(7), dma(7), dma(7), dma(7),
        dma(3), dma(3), dma(7), dma(7), dma(8), dma(8),
    ]
    any_space = pl.BlockSpec(memory_space=pl.ANY)
    in_vmem = pl.BlockSpec(memory_space=pltpu.VMEM)
    field, fin = pl.pallas_call(
        kernel,
        out_shape=(
            jax.ShapeDtypeStruct((TOK, WIDTH), BF16),
            jax.ShapeDtypeStruct((2, CHUNKS, TILES, 16, 128), BF16),
        ),
        in_specs=[any_space] * 10,
        out_specs=(in_vmem,) * 2,
        scratch_shapes=scratch,
        compiler_params=pltpu.CompilerParams(
            collective_id=0, has_side_effects=True, vmem_limit_bytes=48 * 2**20),
        name="window_backward",
    )(
        *[pltpu.with_memory_space_constraint(o, pltpu.HBM) for o in (grid_state.reshape(TOK, WIDTH), cotangent.reshape(TOK, WIDTH),
        mask_ids.transpose(1, 0, 2), earth_bias.transpose(1, 2, 3, 0, 4).reshape(864, 2, 23),
        qkv_weight, proj_weight, *tables)]
    )
    field, gqkv, gproj, gbias = pl.pallas_call(
        unpack,
        out_shape=(
            jax.ShapeDtypeStruct((TOK, WIDTH), BF16),
            jax.ShapeDtypeStruct((192, 576), F32),
            jax.ShapeDtypeStruct((192, 192), F32),
            jax.ShapeDtypeStruct((864, 2, 23), F32),
        ),
        in_specs=[in_vmem] * 2,
        out_specs=(any_space,) * 4,
        scratch_shapes=[vm((192, 576), F32), vm((192, 192), F32), vm((864, 2, 23), F32), dma(4)],
        compiler_params=pltpu.CompilerParams(vmem_limit_bytes=16 * 2**20),
        name="unpack",
    )(field, fin)
    gbias = gbias.reshape(6, 12, 12, 2, 23).transpose(3, 0, 1, 2, 4)
    return field.reshape(grid_state.shape), gqkv, gproj, gbias


def solution(mesh):
    placed = (
        P(None, "lat", "lon", None),
        P(None, "lat", "lon", None),
        P(None, "lat", "lon"),
        P(),
        P(),
        P(),
    )
    return jax.shard_map(
        body,
        mesh=mesh,
        in_specs=placed,
        out_specs=(P(None, "lat", "lon", None), P(), P(), P()),
        check_vma=False,
    )
```

```python
import functools

import jax
import jax.numpy as jnp
import numpy as np
from jax import lax
from jax.experimental import pallas as pl
from jax.experimental.pallas import tpu as pltpu
from jax.sharding import PartitionSpec as P

MESH = pl.DeviceIdType.MESH
F32, BF16 = jnp.float32, jnp.bfloat16

TOK = 288
WIN = 144
WIDTH = 192
HEADS = 6
SWAP, EAST, CORNER, ALL = 288, 400, 448, 496
STRIPS = ((0, SWAP, 112), (112, EAST, 48), (160, CORNER, 48))
SENT = 208
CHUNKS, TILES = 8, 6
HALF = 36
MAIN = HALF // TILES
ROWS_MAIN, COLS_MAIN = 12, 6
PACKS = (5, 5, 2)


def build_tables():
    natural = lambda z, r, c: (z * 6 + r) * 24 + c
    send = np.zeros((SENT, TOK), np.float32)
    for z in range(2):
        for r in range(3):
            row = z * 3 + r
            for c in range(18):
                send[row * 18 + c, natural(z, r, c + 6)] = 1
            for c in range(6):
                send[112 + row * 6 + c, natural(z, r + 3, c)] = 1
                send[160 + row * 6 + c, natural(z, r, c)] = 1
    frame = np.zeros((TOK, ALL), np.float32)
    id_rows = np.zeros((TOK, 64), np.float32)
    id_cols = np.zeros((TOK, 128), np.float32)
    wrapped = np.zeros((TOK, 128), np.float32)
    for w in range(2):
        for z in range(2):
            for r in range(6):
                for p in range(12):
                    t = w * WIN + (z * 6 + r) * 12 + p
                    c = w * 12 + p
                    above = z * 3 + r - 3
                    if r < 3 and c < 18:
                        src, block, row, col = natural(z, r + 3, c + 6), 0, r + 3, c + 6
                    elif r < 3:
                        src, block, row, col = EAST + (z * 3 + r) * 6 + c - 18, 2, r + 3, c - 18
                    elif c < 18:
                        src, block, row, col = SWAP + above * 18 + c, 1, r - 3, c + 6
                    else:
                        src, block, row, col = CORNER + above * 6 + c - 18, 3, r - 3, c - 18
                    frame[t, src] = 1
                    id_rows[t, block * 16 + row * 2 + z] = 1
                    id_cols[t, col] = 1
                    wrapped[t, :] = 3.0 if r >= 3 else 0.0
    back = frame[:, TOK:].T
    out = np.concatenate([frame[:, :TOK].T, send.T], axis=1)
    spread = np.zeros((384, 1792), np.float32)
    for x in range(12):
        for b in range(12):
            for y in range(12):
                key = b * 12 + y
                col = x * 128 + key if key < 128 else 1536 + x * 16 + key - 128
                spread[(b // 5) * 128 + (b % 5) * 24 + x - y + 11, col] = 1
    cells = np.concatenate([send, back], axis=0)
    moves = np.concatenate([frame, out], axis=0)
    ids = np.concatenate([id_rows, np.zeros((TOK, 64), np.float32), id_cols, wrapped], axis=1)
    return [np.asarray(t, jnp.bfloat16) for t in (cells, moves, ids, spread)]


def mm(a, b):
    return lax.dot_general(a, b, (((1,), (0,)), ((), ())), preferred_element_type=F32)


def mm_nt(a, b):
    return lax.dot_general(a, b, (((1,), (1,)), ((), ())), preferred_element_type=F32)


def mm_tn(a, b):
    return lax.dot_general(a, b, (((0,), (0,)), ((), ())), preferred_element_type=F32)


def main_place(t):
    return t // HALF, (t % HALF) // TILES, t % TILES


def bias_place(t):
    return (HALF + t) // TILES, t % TILES


def roll(a, shift):
    shift %= 128
    return pltpu.roll(a, shift, 1) if shift else a


def kernel(
    x_hbm, cot_hbm, ids_hbm, eb_hbm, wqkv_hbm, wproj_hbm, cells_hbm, moves_hbm, idt_hbm, spread_hbm,
    field_ref, fin,
    x_v, cot_v, ids_v, eb_v, wqkv_v, wproj_v, cells_v, moves_v, idt_v, spread_v,
    xc, send_b, idb, fa, fb, ba, bb, gback, ret_b, wqkv_t,
    pay, rc, cur, ra, ry, rz,
    in_sem, h_ss, h_rs, r_ss, r_rs, c_ss, c_rs, a_ss, a_rs, y_ss, y_rs, z_ss, z_rs,
    g_ss, g_rs, k_ss, k_rs,
):
    lat, lon = lax.axis_index("lat"), lax.axis_index("lon")
    iy, ix, izl = lat // 8, (lat // 2) % 4, lat % 2
    izh, core = lon // 2, lon % 2
    iz = izh * 2 + izl
    band = izl

    lat_o = lat + 1 - 2 * izl
    east, west = (lon + 1) % 8, (lon + 7) % 8
    sibling = (lat, izh * 2 + 1 - core)

    def pick(a, b):
        return a * (1 - core) + b * core

    def member(g):
        return (pick(iy * 8 + g, g * 8 + ix * 2 + izl), lon)

    def second(i):
        return (pick(i * 8 + ix * 2 + izl, iy * 8 + ix * 2 + i % 2), pick(lon, (i // 2) * 2 + core))

    def third(i):
        return (pick(lat, iy * 8 + i * 2 + izl), pick(i * 2 + core, lon))

    group, place2, place3 = pick(ix * 2 + izl, iy), pick(iy, iz), pick(izh, ix)
    far8, far4 = (4, 3, 5, 2, 6, 1, 7), (2, 1, 3)
    turns = ((2, 1), (1, 1), (3, 1), (2, 0), (1, 0), (3, 0), (0, 1))

    def first_to(i, way):
        dx, dz = turns[i]
        to_x, to_z = (ix + way * dx + 4) % 4, (izl + dz) % 2
        return pick(to_x * 2 + to_z, (iy + way * far8[i] + 8) % 8)

    to_first = [first_to(i, 1) for i in range(7)]
    from_first = [first_to(i, -1) for i in range(7)]
    to_second = [(place2 + d) % 8 for d in far8]
    to_third = [(place3 + d) % 4 for d in far4]

    srcs = [x_hbm, cot_hbm, cells_hbm, ids_hbm, eb_hbm, spread_hbm, moves_hbm, idt_hbm,
            wqkv_hbm, wproj_hbm]
    dsts = [x_v, cot_v, cells_v, ids_v, eb_v, spread_v, moves_v, idt_v, wqkv_v, wproj_v]
    loads = [pltpu.make_async_copy(s, d, in_sem.at[i]) for i, (s, d) in enumerate(zip(srcs, dsts))]
    for cp in loads[:4]:
        cp.start()

    barrier = pltpu.get_barrier_semaphore()
    partners = [(lat_o, lon), (lat, west), (lat, east), (lat_o, west), (lat_o, east), sibling]
    partners += [member(j) for j in to_first]
    partners += [second(j) for j in to_second]
    partners += [third(j) for j in to_third]
    for p in partners:
        pl.semaphore_signal(barrier, inc=1, device_id=p, device_id_type=MESH)
    for cp in loads[4:]:
        cp.start()

    loads[0].wait()
    loads[1].wait()
    loads[2].wait()
    loads[3].wait()
    xc[0:TOK, 0:128] = x_v[:, 0:128]
    xc[0:TOK, 128:256] = cot_v[:, 0:128]
    xc[0:TOK, 256:384] = jnp.concatenate([x_v[:, 128:192], cot_v[:, 128:192]], axis=1)
    send_b[...] = mm(cells_v[0:SENT, :], xc[0:TOK, :]).astype(BF16)
    rows_id = jnp.concatenate([ids_v.reshape(12, 24)[...].astype(F32), jnp.zeros((4, 24), F32)], axis=0)
    idb[0] = jnp.concatenate([rows_id, jnp.zeros((16, 104), F32)], axis=1).astype(BF16)

    pl.semaphore_wait(barrier, len(partners))

    def remote(src, dst, ss, rs, dev):
        return pltpu.make_async_remote_copy(
            src_ref=src, dst_ref=dst, send_sem=ss, recv_sem=rs, device_id=dev, device_id_type=MESH)

    strip_to = [(lat_o, lon), (lat, west), (lat_o, west)]
    id_to = [(lat_o, lon), (lat, west), (lat_o, west)]
    strips = [remote(send_b.at[pl.ds(a, n)], xc.at[pl.ds(b, n)], h_ss.at[i], h_rs.at[i], strip_to[i])
              for i, (a, b, n) in enumerate(STRIPS)]
    id_blocks = [remote(idb.at[0], idb.at[i + 1], h_ss.at[3 + i], h_rs.at[3 + i], id_to[i])
                 for i in range(3)]
    halo = [strips[2], strips[0], strips[1]] + id_blocks
    for cp in halo:
        cp.start()

    loads[4].wait()
    loads[5].wait()
    eb_rows = eb_v.reshape(1728, 23)
    nothing = jnp.zeros((72, 105), F32)
    packs = []
    for g in range(3):
        acc = None
        for k in range(PACKS[g]):
            part = eb_rows[pl.ds(2 * (5 * g + k) + band, 72, stride=24), :]
            part = roll(jnp.concatenate([part, nothing], axis=1), 24 * k)
            acc = part if acc is None else acc + part
        packs.append(acc)
    e = jnp.concatenate(packs, axis=1)
    hi = e.astype(BF16)
    rest = e - hi.astype(F32)
    mid = rest.astype(BF16)
    low = (rest - mid.astype(F32)).astype(BF16)
    full = (mm(hi, spread_v[...]) + mm(mid, spread_v[...])) + mm(low, spread_v[...])
    for x in range(12):
        fa[pl.ds(x, 72, stride=12), :] = full[:, x * 128:(x + 1) * 128]
        tail = full[:, 1536 + (x // 8) * 128:1664 + (x // 8) * 128]
        fb[pl.ds(x, 72, stride=12), :] = roll(tail, -16 * x)

    for cp in loads[6:]:
        cp.wait()
    wqkv_t[...] = wqkv_v[...].astype(F32).T.astype(BF16)
    lane_head = lax.broadcasted_iota(jnp.int32, (WIN, WIDTH), 1) // 32
    classes = lax.broadcasted_iota(jnp.int32, (TOK, 128), 1).astype(F32)
    scale = 32.0 ** (-0.5)
    for cp in halo:
        cp.wait_recv()

    fr = mm(moves_v[0:TOK, :], xc[...])
    xf = jnp.concatenate([fr[:, 0:128], fr[:, 256:320]], axis=1)
    cot_f = jnp.concatenate([fr[:, 128:256], fr[:, 320:384]], axis=1)
    cot = cot_f.astype(BF16)
    mean = jnp.sum(xf, axis=1, keepdims=True) * (1.0 / WIDTH)
    xm = xf - mean
    var = jnp.sum(xm * xm, axis=1, keepdims=True) * (1.0 / WIDTH)
    rdev = lax.rsqrt(var + 1e-05)
    xhat = xm * rdev
    normed = xhat.astype(BF16)
    q = mm(normed, wqkv_v[:, 0:192]).astype(BF16)
    da = mm_nt(cot, wproj_v[...]).astype(BF16)

    id_all = jnp.concatenate([idb[i] for i in range(4)], axis=0)
    id_row = mm(idt_v[:, 0:64], id_all) * idt_v[:, 128:256].astype(F32)
    id_cell = mm(id_row.astype(BF16), jnp.ones((128, 128), BF16))
    key = id_cell + idt_v[:, 256:384].astype(F32) * izl.astype(F32)
    onehot = jnp.where(key == classes, 1.0, 0.0).astype(BF16)

    def spread_heads(a):
        zero = jnp.zeros((WIN, WIDTH), BF16)
        return jnp.concatenate([jnp.where(lane_head == h, a, zero) for h in range(HEADS)], axis=0)

    def each_head(dot, a, b):
        parts = [dot(a[h * 32:(h + 1) * 32], b[h * WIN:(h + 1) * WIN]) for h in range(HEADS)]
        return jnp.concatenate(parts, axis=0)

    g_qkv = g_proj = None
    d_qkv_t = []
    for w in range(2):
        rows = slice(w * WIN, (w + 1) * WIN)
        normed_t = xhat[rows].T.astype(BF16)
        qkv_t = mm_nt(wqkv_t[...], normed[rows]).astype(BF16)
        q_t, k_t, v_t = qkv_t[0:192], qkv_t[192:384], qkv_t[384:576]
        da_t = mm_nt(wproj_v[...], cot[rows]).astype(BF16)
        block = (mm_nt(onehot[rows], onehot[rows]) - 1.0) * 1e30
        bias = jnp.concatenate([fa[...], fb[:, 0:16]], axis=1)
        s = mm(spread_heads(q[rows]), k_t) * scale + bias + jnp.concatenate([block] * HEADS, axis=0)
        ex = jnp.exp(s - jnp.max(s, axis=1, keepdims=True))
        p = ex * (1.0 / jnp.sum(ex, axis=1, keepdims=True))
        pb = p.astype(BF16)
        dp = mm(spread_heads(da[rows]), v_t)
        ds = p * (dp - jnp.sum(p * dp, axis=1, keepdims=True))
        dsb = ds.astype(BF16)
        ds_a = ds[:, 0:128]
        ds_b = jnp.concatenate([ds[:, 128:144], jnp.zeros((HEADS * WIN, 112), F32)], axis=1)
        if w == 0:
            ba[...] = ds_a
            bb[...] = ds_b
        else:
            ba[...] += ds_a
            bb[...] += ds_b
        att_t = each_head(mm_nt, v_t, pb).astype(BF16)
        dq_t = (each_head(mm_nt, k_t, dsb) * scale).astype(BF16)
        dk_t = (each_head(mm, q_t, dsb) * scale).astype(BF16)
        dv_t = each_head(mm, da_t, pb).astype(BF16)
        d_qkv_t.append(jnp.concatenate([dq_t, dk_t, dv_t], axis=0))
        w_qkv, w_proj = mm_nt(normed_t, d_qkv_t[w]), mm(att_t, cot[rows])
        g_qkv = w_qkv if w == 0 else g_qkv + w_qkv
        g_proj = w_proj if w == 0 else g_proj + w_proj

    g_mix = jnp.concatenate([g_qkv[:, 512:576], g_proj[:, 128:192]], axis=1)
    columns = [g_qkv[:, j * 128:(j + 1) * 128] for j in range(4)] + [g_mix, g_proj[:, 0:128]]
    for i in range(ROWS_MAIN):
        for j in range(COLS_MAIN):
            pay[main_place(i * COLS_MAIN + j)] = columns[j][i * 16:(i + 1) * 16].astype(BF16)
    cores = [remote(pay.at[1 - core, pl.ds(0, MAIN)], rc.at[pl.ds(0, MAIN)], c_ss.at[0], c_rs.at[0], sibling)]
    cores[0].start()

    mains, tails = [], [None, None]
    for x in range(12):
        mains.append(ba[pl.ds(x, 72, stride=12), :])
        t = roll(bb[pl.ds(x, 72, stride=12), :], 16 * x)
        tails[x // 8] = t if tails[x // 8] is None else tails[x // 8] + t
    terms = jnp.concatenate(mains + tails, axis=1)
    t_hi = terms.astype(BF16)
    t_lo = (terms - t_hi.astype(F32)).astype(BF16)
    gb = mm_nt(t_hi, spread_v[...]) + mm_nt(t_lo, spread_v[...])
    g0, g1, g2 = gb[:, 0:128], gb[:, 128:256], gb[:, 256:384]
    rest = jnp.concatenate([roll(g2[40:72], 64), jnp.zeros((8, 128), F32)], axis=0)
    packed = jnp.concatenate([g0, g1[64:72], g1[0:64], g2[0:40] + rest, jnp.zeros((8, 128), F32)], axis=0)
    for which in range(2):
        mine = jnp.where(band == which, packed, 0.0).astype(BF16)
        for t in range(12):
            pay[(which, *bias_place(t))] = mine[t * 16:(t + 1) * 16]
    rest_of = pl.ds(MAIN, CHUNKS - MAIN)
    cores.append(remote(pay.at[1 - core, rest_of], rc.at[rest_of], c_ss.at[1], c_rs.at[1], sibling))
    cores[1].start()

    for cp in cores:
        cp.wait_recv()
    scatter = []
    for d, j in enumerate(to_first + [group]):
        cur[j] = (pay[core, j].astype(F32) + rc[j].astype(F32)).astype(BF16)
        if d < 7:
            cp = remote(cur.at[j], ra.at[group], a_ss.at[d], a_rs.at[d], member(j))
            cp.start()
            scatter.append(cp)
    ra[group] = cur[group]

    dn = jnp.concatenate([mm_tn(d, wqkv_t[...]) for d in d_qkv_t], axis=0)
    m1 = jnp.sum(dn, axis=1, keepdims=True) * (1.0 / WIDTH)
    m2 = jnp.sum(dn * xhat, axis=1, keepdims=True) * (1.0 / WIDTH)
    gf = (cot_f + rdev * (dn - m1 - xhat * m2)).astype(BF16)
    gback[0:TOK, :] = gf
    ret_b[...] = mm(cells_v[SENT:2 * SENT, :], gf).astype(BF16)
    ret_to = [(lat_o, lon), (lat, east), (lat_o, east)]
    returns = [remote(ret_b.at[pl.ds(a, n)], gback.at[pl.ds(b, n)], r_ss.at[i], r_rs.at[i], ret_to[i])
               for i, (a, b, n) in enumerate(STRIPS)]
    for cp in returns:
        cp.start()

    def total(ref, n):
        acc = ref[0].astype(F32)
        for i in range(1, n):
            acc = acc + ref[i].astype(F32)
        return acc.astype(BF16)

    for cp in scatter:
        cp.wait_recv()
    ry[place2] = total(ra, 8)
    over_y = [remote(ry.at[place2], ry.at[place2], y_ss.at[i], y_rs.at[i], second(j))
              for i, j in enumerate(to_second)]
    for cp in over_y:
        cp.start()

    for cp in returns:
        cp.wait_recv()
    field_ref[...] = mm(moves_v[TOK:2 * TOK, :], gback[...]).astype(BF16)

    for cp in over_y:
        cp.wait_recv()
    rz[place3] = total(ry, 8)
    over_z = [remote(rz.at[place3], rz.at[place3], z_ss.at[i], z_rs.at[i], third(j))
              for i, j in enumerate(to_third)]
    for cp in over_z:
        cp.start()
    for cp in over_z:
        cp.wait_recv()

    fin[core, group] = total(rz, 4)
    gather = [remote(fin.at[core, group], fin.at[core, group], g_ss.at[i], g_rs.at[i], member(j))
              for i, j in enumerate(to_first)]
    for cp in gather:
        cp.start()
    final = []
    for i in (7, 6, 5, 4, 3, 2, 1, 0):
        if i < 7:
            gather[i].wait_recv()
        j = group if i == 7 else from_first[i]
        cp = remote(fin.at[core, j], fin.at[core, j], k_ss.at[i], k_rs.at[i], sibling)
        cp.start()
        final.append(cp)
    for cp in final:
        cp.wait_recv()
    for cp in halo + returns + cores + scatter + over_y + over_z + gather + final:
        cp.wait_send()


def unpack(field_in, fin, field_hbm, gqkv_hbm, gproj_hbm, gbias_hbm, gqkv_ref, gproj_ref, gbias_ref, sem):
    outs = [(field_in, field_hbm), (gqkv_ref, gqkv_hbm), (gproj_ref, gproj_hbm), (gbias_ref, gbias_hbm)]
    stores = [pltpu.make_async_copy(src, dst, sem.at[i]) for i, (src, dst) in enumerate(outs)]
    stores[0].start()
    token_scale = 147456.0 ** (-0.5)
    for i in range(ROWS_MAIN):
        r = slice(i * 16, (i + 1) * 16)
        row = [fin[main_place(i * COLS_MAIN + j)].astype(F32) * token_scale for j in range(COLS_MAIN)]
        for j in range(4):
            gqkv_ref[r, j * 128:(j + 1) * 128] = row[j]
        gqkv_ref[r, 512:576] = row[4][:, 0:64]
        gproj_ref[r, 0:128] = row[5]
        gproj_ref[r, 128:192] = row[4][:, 64:128]
    stores[1].start()
    stores[2].start()
    bias_rows = gbias_ref.reshape(1728, 23)
    for which in range(2):
        packed = jnp.concatenate([fin[(which, *bias_place(t))] for t in range(12)], axis=0).astype(F32)
        rest = packed[144:184]
        cols = [packed[0:72], jnp.concatenate([packed[80:144], packed[72:80]], axis=0),
                jnp.concatenate([rest, roll(rest[0:32], -64)], axis=0)]
        for g in range(3):
            for k in range(PACKS[g]):
                place = pl.ds(2 * (5 * g + k) + which, 72, stride=24)
                bias_rows[place, :] = roll(cols[g], -24 * k)[:, 0:23]
    stores[3].start()
    for cp in stores:
        cp.wait()


def body(grid_state, cotangent, mask_ids, earth_bias, qkv_weight, proj_weight):
    tables = [jnp.asarray(t) for t in build_tables()]
    vm = pltpu.VMEM
    dma = lambda n: pltpu.SemaphoreType.DMA((n,))
    tiles = lambda *n: vm((*n, 16, 128), BF16)
    scratch = [
        vm((TOK, WIDTH), BF16), vm((TOK, WIDTH), BF16), vm((6, 2, 24), jnp.int32),
        vm((864, 2, 23), F32), vm((192, 576), BF16), vm((192, 192), BF16),
        vm((2 * SENT, TOK), BF16), vm((2 * TOK, ALL), BF16), vm((TOK, 384), BF16),
        vm((384, 1792), BF16),
        vm((ALL, 384), BF16), vm((SENT, 384), BF16), vm((4, 16, 128), BF16),
        vm((864, 128), F32), vm((864, 128), F32), vm((864, 128), F32), vm((864, 128), F32),
        vm((ALL, WIDTH), BF16), vm((SENT, WIDTH), BF16), vm((576, WIDTH), BF16),
        tiles(2, CHUNKS, TILES), tiles(CHUNKS, TILES), tiles(CHUNKS, TILES), tiles(8, TILES), tiles(8, TILES), tiles(4, TILES),
        dma(10), dma(6), dma(6), dma(3), dma(3), dma(2), dma(2), dma(7), dma(7), dma(7), dma(7),
        dma(3), dma(3), dma(7), dma(7), dma(8), dma(8),
    ]
    any_space = pl.BlockSpec(memory_space=pl.ANY)
    in_vmem = pl.BlockSpec(memory_space=pltpu.VMEM)
    field, fin = pl.pallas_call(
        kernel,
        out_shape=(
            jax.ShapeDtypeStruct((TOK, WIDTH), BF16),
            jax.ShapeDtypeStruct((2, CHUNKS, TILES, 16, 128), BF16),
        ),
        in_specs=[any_space] * 10,
        out_specs=(in_vmem,) * 2,
        scratch_shapes=scratch,
        compiler_params=pltpu.CompilerParams(
            collective_id=0, has_side_effects=True, vmem_limit_bytes=48 * 2**20),
        name="window_backward",
    )(
        *[pltpu.with_memory_space_constraint(o, pltpu.HBM) for o in (grid_state.reshape(TOK, WIDTH), cotangent.reshape(TOK, WIDTH),
        mask_ids.transpose(1, 0, 2), earth_bias.transpose(1, 2, 3, 0, 4).reshape(864, 2, 23),
        qkv_weight, proj_weight, *tables)]
    )
    field, gqkv, gproj, gbias = pl.pallas_call(
        unpack,
        out_shape=(
            jax.ShapeDtypeStruct((TOK, WIDTH), BF16),
            jax.ShapeDtypeStruct((192, 576), F32),
            jax.ShapeDtypeStruct((192, 192), F32),
            jax.ShapeDtypeStruct((864, 2, 23), F32),
        ),
        in_specs=[in_vmem] * 2,
        out_specs=(any_space,) * 4,
        scratch_shapes=[vm((192, 576), F32), vm((192, 192), F32), vm((864, 2, 23), F32), dma(4)],
        compiler_params=pltpu.CompilerParams(vmem_limit_bytes=16 * 2**20),
        name="unpack",
    )(field, fin)
    gbias = gbias.reshape(6, 12, 12, 2, 23).transpose(3, 0, 1, 2, 4)
    return field.reshape(grid_state.shape), gqkv, gproj, gbias


def solution(mesh):
    placed = (
        P(None, "lat", "lon", None),
        P(None, "lat", "lon", None),
        P(None, "lat", "lon"),
        P(),
        P(),
        P(),
    )
    return jax.shard_map(
        body,
        mesh=mesh,
        in_specs=placed,
        out_specs=(P(None, "lat", "lon", None), P(), P(), P()),
        check_vma=False,
    )
```

```python
import functools

import jax
import jax.numpy as jnp
import numpy as np
from jax import lax
from jax.experimental import pallas as pl
from jax.experimental.pallas import tpu as pltpu
from jax.sharding import PartitionSpec as P

MESH = pl.DeviceIdType.MESH
F32, BF16 = jnp.float32, jnp.bfloat16

TOK = 288
WIN = 144
WIDTH = 192
HEADS = 6
SWAP, EAST, CORNER, ALL = 288, 400, 448, 496
STRIPS = ((0, SWAP, 112), (112, EAST, 48), (160, CORNER, 48))
SENT = 208
CHUNKS, TILES = 8, 6
HALF = 36
MAIN = HALF // TILES
ROWS_MAIN, COLS_MAIN = 12, 6
PAD = 880
PACKS = (5, 5, 2)


def build_tables():
    natural = lambda z, r, c: (z * 6 + r) * 24 + c
    send = np.zeros((SENT, TOK), np.float32)
    for z in range(2):
        for r in range(3):
            row = z * 3 + r
            for c in range(18):
                send[row * 18 + c, natural(z, r, c + 6)] = 1
            for c in range(6):
                send[112 + row * 6 + c, natural(z, r + 3, c)] = 1
                send[160 + row * 6 + c, natural(z, r, c)] = 1
    frame = np.zeros((TOK, ALL), np.float32)
    id_rows = np.zeros((TOK, 64), np.float32)
    id_cols = np.zeros((TOK, 128), np.float32)
    wrapped = np.zeros((TOK, 128), np.float32)
    for w in range(2):
        for z in range(2):
            for r in range(6):
                for p in range(12):
                    t = w * WIN + (z * 6 + r) * 12 + p
                    c = w * 12 + p
                    above = z * 3 + r - 3
                    if r < 3 and c < 18:
                        src, block, row, col = natural(z, r + 3, c + 6), 0, r + 3, c + 6
                    elif r < 3:
                        src, block, row, col = EAST + (z * 3 + r) * 6 + c - 18, 2, r + 3, c - 18
                    elif c < 18:
                        src, block, row, col = SWAP + above * 18 + c, 1, r - 3, c + 6
                    else:
                        src, block, row, col = CORNER + above * 6 + c - 18, 3, r - 3, c - 18
                    frame[t, src] = 1
                    id_rows[t, block * 16 + row * 2 + z] = 1
                    id_cols[t, col] = 1
                    wrapped[t, :] = 3.0 if r >= 3 else 0.0
    back = frame[:, TOK:].T
    out = np.concatenate([frame[:, :TOK].T, send.T], axis=1)
    spread = np.zeros((384, 1792), np.float32)
    for x in range(12):
        for b in range(12):
            for y in range(12):
                key = b * 12 + y
                col = x * 128 + key if key < 128 else 1536 + x * 16 + key - 128
                spread[(b // 5) * 128 + (b % 5) * 24 + x - y + 11, col] = 1
    cells = np.concatenate([send, back], axis=0)
    moves = np.concatenate([frame, out], axis=0)
    ids = np.concatenate([id_rows, np.zeros((TOK, 64), np.float32), id_cols, wrapped], axis=1)
    return [np.asarray(t, jnp.bfloat16) for t in (cells, moves, ids, spread)]


def mm(a, b):
    return lax.dot_general(a, b, (((1,), (0,)), ((), ())), preferred_element_type=F32)


def mm_nt(a, b):
    return lax.dot_general(a, b, (((1,), (1,)), ((), ())), preferred_element_type=F32)


def mm_tn(a, b):
    return lax.dot_general(a, b, (((0,), (0,)), ((), ())), preferred_element_type=F32)


def main_place(t):
    return t // HALF, (t % HALF) // TILES, t % TILES


def bias_place(t):
    return (HALF + t) // TILES, t % TILES


def roll(a, shift):
    shift %= 128
    return pltpu.roll(a, shift, 1) if shift else a


def kernel(
    x_hbm, cot_hbm, ids_hbm, eb_hbm, wqkv_hbm, wproj_hbm, cells_hbm, moves_hbm, idt_hbm, spread_hbm,
    field_ref, fin,
    x_v, cot_v, ids_v, eb_v, wqkv_v, wproj_v, cells_v, moves_v, idt_v, spread_v,
    xc, send_b, idb, fa, fb, ba, bb, gback, ret_b, wqkv_t,
    pay, rc, cur, ra, ry, rz,
    in_sem, h_ss, h_rs, r_ss, r_rs, c_ss, c_rs, a_ss, a_rs, y_ss, y_rs, z_ss, z_rs,
    g_ss, g_rs, k_ss, k_rs,
):
    lat, lon = lax.axis_index("lat"), lax.axis_index("lon")
    iy, ix, izl = lat // 8, (lat // 2) % 4, lat % 2
    izh, core = lon // 2, lon % 2
    iz = izh * 2 + izl
    band = izl

    lat_o = lat + 1 - 2 * izl
    east, west = (lon + 1) % 8, (lon + 7) % 8
    sibling = (lat, izh * 2 + 1 - core)

    def pick(a, b):
        return a * (1 - core) + b * core

    def member(g):
        return (pick(iy * 8 + g, g * 8 + ix * 2 + izl), lon)

    def second(i):
        return (pick(i * 8 + ix * 2 + izl, iy * 8 + ix * 2 + i % 2), pick(lon, (i // 2) * 2 + core))

    def third(i):
        return (pick(lat, iy * 8 + i * 2 + izl), pick(i * 2 + core, lon))

    group, place2, place3 = pick(ix * 2 + izl, iy), pick(iy, iz), pick(izh, ix)
    far8, far4 = (4, 3, 5, 2, 6, 1, 7), (2, 1, 3)
    turns = ((2, 1), (1, 1), (3, 1), (2, 0), (1, 0), (3, 0), (0, 1))

    def first_to(i, way):
        dx, dz = turns[i]
        to_x, to_z = (ix + way * dx + 4) % 4, (izl + dz) % 2
        return pick(to_x * 2 + to_z, (iy + way * far8[i] + 8) % 8)

    to_first = [first_to(i, 1) for i in range(7)]
    from_first = [first_to(i, -1) for i in range(7)]
    to_second = [(place2 + d) % 8 for d in far8]
    to_third = [(place3 + d) % 4 for d in far4]

    srcs = [x_hbm, cot_hbm, cells_hbm, ids_hbm, eb_hbm, spread_hbm, moves_hbm, idt_hbm,
            wqkv_hbm, wproj_hbm]
    dsts = [x_v, cot_v, cells_v, ids_v, eb_v.at[pl.ds(0, 864)], spread_v, moves_v, idt_v, wqkv_v, wproj_v]
    loads = [pltpu.make_async_copy(s, d, in_sem.at[i]) for i, (s, d) in enumerate(zip(srcs, dsts))]
    for cp in loads[:4]:
        cp.start()

    barrier = pltpu.get_barrier_semaphore()
    partners = [(lat_o, lon), (lat, west), (lat, east), (lat_o, west), (lat_o, east), sibling]
    partners += [member(j) for j in to_first]
    partners += [second(j) for j in to_second]
    partners += [third(j) for j in to_third]
    for p in partners:
        pl.semaphore_signal(barrier, inc=1, device_id=p, device_id_type=MESH)
    for cp in loads[4:]:
        cp.start()

    loads[0].wait()
    loads[1].wait()
    loads[2].wait()
    loads[3].wait()
    xc[0:TOK, 0:128] = x_v[:, 0:128]
    xc[0:TOK, 128:256] = cot_v[:, 0:128]
    xc[0:TOK, 256:384] = jnp.concatenate([x_v[:, 128:192], cot_v[:, 128:192]], axis=1)
    send_b[...] = mm(cells_v[0:SENT, :], xc[0:TOK, :]).astype(BF16)
    rows_id = jnp.concatenate([ids_v.reshape(12, 24)[...].astype(F32), jnp.zeros((4, 24), F32)], axis=0)
    idb[0] = jnp.concatenate([rows_id, jnp.zeros((16, 104), F32)], axis=1).astype(BF16)

    pl.semaphore_wait(barrier, len(partners))

    def remote(src, dst, ss, rs, dev):
        return pltpu.make_async_remote_copy(
            src_ref=src, dst_ref=dst, send_sem=ss, recv_sem=rs, device_id=dev, device_id_type=MESH)

    strip_to = [(lat_o, lon), (lat, west), (lat_o, west)]
    id_to = [(lat_o, lon), (lat, west), (lat_o, west)]
    strips = [remote(send_b.at[pl.ds(a, n)], xc.at[pl.ds(b, n)], h_ss.at[i], h_rs.at[i], strip_to[i])
              for i, (a, b, n) in enumerate(STRIPS)]
    id_blocks = [remote(idb.at[0], idb.at[i + 1], h_ss.at[3 + i], h_rs.at[3 + i], id_to[i])
                 for i in range(3)]
    halo = [strips[2], strips[0], strips[1]] + id_blocks
    for cp in halo:
        cp.start()

    loads[4].wait()
    loads[5].wait()
    eb_rows = eb_v.reshape(2 * PAD, 23)
    nothing = jnp.zeros((72, 105), F32)
    packs = []
    for g in range(3):
        acc = None
        for k in range(PACKS[g]):
            part = eb_rows[pl.ds(2 * (5 * g + k) + band, 72, stride=24), :]
            part = roll(jnp.concatenate([part, nothing], axis=1), 24 * k)
            acc = part if acc is None else acc + part
        packs.append(acc)
    e = jnp.concatenate(packs, axis=1)
    hi = e.astype(BF16)
    rest = e - hi.astype(F32)
    mid = rest.astype(BF16)
    low = (rest - mid.astype(F32)).astype(BF16)
    full = (mm(hi, spread_v[...]) + mm(mid, spread_v[...])) + mm(low, spread_v[...])
    for x in range(12):
        fa[pl.ds(x, 72, stride=12), :] = full[:, x * 128:(x + 1) * 128]
        tail = full[:, 1536 + (x // 8) * 128:1664 + (x // 8) * 128]
        fb[pl.ds(x, 72, stride=12), :] = roll(tail, -16 * x)

    for cp in loads[6:]:
        cp.wait()
    wqkv_t[...] = wqkv_v[...].astype(F32).T.astype(BF16)
    lane_head = lax.broadcasted_iota(jnp.int32, (WIN, WIDTH), 1) // 32
    classes = lax.broadcasted_iota(jnp.int32, (TOK, 128), 1).astype(F32)
    scale = 32.0 ** (-0.5)
    for cp in halo:
        cp.wait_recv()

    fr = mm(moves_v[0:TOK, :], xc[...])
    xf = jnp.concatenate([fr[:, 0:128], fr[:, 256:320]], axis=1)
    cot_f = jnp.concatenate([fr[:, 128:256], fr[:, 320:384]], axis=1)
    cot = cot_f.astype(BF16)
    mean = jnp.sum(xf, axis=1, keepdims=True) * (1.0 / WIDTH)
    xm = xf - mean
    var = jnp.sum(xm * xm, axis=1, keepdims=True) * (1.0 / WIDTH)
    rdev = lax.rsqrt(var + 1e-05)
    xhat = xm * rdev
    normed = xhat.astype(BF16)
    q = mm(normed, wqkv_v[:, 0:192]).astype(BF16)
    da = mm_nt(cot, wproj_v[...]).astype(BF16)

    id_all = jnp.concatenate([idb[i] for i in range(4)], axis=0)
    id_row = mm(idt_v[:, 0:64], id_all) * idt_v[:, 128:256].astype(F32)
    id_cell = mm(id_row.astype(BF16), jnp.ones((128, 128), BF16))
    key = id_cell + idt_v[:, 256:384].astype(F32) * izl.astype(F32)
    onehot = jnp.where(key == classes, 1.0, 0.0).astype(BF16)

    def spread_heads(a):
        zero = jnp.zeros((WIN, WIDTH), BF16)
        return jnp.concatenate([jnp.where(lane_head == h, a, zero) for h in range(HEADS)], axis=0)

    def each_head(dot, a, b):
        parts = [dot(a[h * 32:(h + 1) * 32], b[h * WIN:(h + 1) * WIN]) for h in range(HEADS)]
        return jnp.concatenate(parts, axis=0)

    g_qkv = g_proj = None
    d_qkv_t = []
    for w in range(2):
        rows = slice(w * WIN, (w + 1) * WIN)
        normed_t = xhat[rows].T.astype(BF16)
        qkv_t = mm_nt(wqkv_t[...], normed[rows]).astype(BF16)
        q_t, k_t, v_t = qkv_t[0:192], qkv_t[192:384], qkv_t[384:576]
        da_t = mm_nt(wproj_v[...], cot[rows]).astype(BF16)
        block = (mm_nt(onehot[rows], onehot[rows]) - 1.0) * 1e30
        bias = jnp.concatenate([fa[0:864, :], fb[0:864, 0:16]], axis=1)
        s = mm(spread_heads(q[rows]), k_t) * scale + bias + jnp.concatenate([block] * HEADS, axis=0)
        ex = jnp.exp(s - jnp.max(s, axis=1, keepdims=True))
        p = ex * (1.0 / jnp.sum(ex, axis=1, keepdims=True))
        pb = p.astype(BF16)
        dp = mm(spread_heads(da[rows]), v_t)
        ds = p * (dp - jnp.sum(p * dp, axis=1, keepdims=True))
        dsb = ds.astype(BF16)
        ds_a = ds[:, 0:128]
        ds_b = jnp.concatenate([ds[:, 128:144], jnp.zeros((HEADS * WIN, 112), F32)], axis=1)
        if w == 0:
            ba[0:864, :] = ds_a
            bb[0:864, :] = ds_b
        else:
            ba[0:864, :] += ds_a
            bb[0:864, :] += ds_b
        att_t = each_head(mm_nt, v_t, pb).astype(BF16)
        dq_t = (each_head(mm_nt, k_t, dsb) * scale).astype(BF16)
        dk_t = (each_head(mm, q_t, dsb) * scale).astype(BF16)
        dv_t = each_head(mm, da_t, pb).astype(BF16)
        d_qkv_t.append(jnp.concatenate([dq_t, dk_t, dv_t], axis=0))
        w_qkv, w_proj = mm_nt(normed_t, d_qkv_t[w]), mm(att_t, cot[rows])
        g_qkv = w_qkv if w == 0 else g_qkv + w_qkv
        g_proj = w_proj if w == 0 else g_proj + w_proj

    g_mix = jnp.concatenate([g_qkv[:, 512:576], g_proj[:, 128:192]], axis=1)
    columns = [g_qkv[:, j * 128:(j + 1) * 128] for j in range(4)] + [g_mix, g_proj[:, 0:128]]
    for i in range(ROWS_MAIN):
        for j in range(COLS_MAIN):
            pay[main_place(i * COLS_MAIN + j)] = columns[j][i * 16:(i + 1) * 16].astype(BF16)
    cores = [remote(pay.at[1 - core, pl.ds(0, MAIN)], rc.at[pl.ds(0, MAIN)], c_ss.at[0], c_rs.at[0], sibling)]
    cores[0].start()

    mains, tails = [], [None, None]
    for x in range(12):
        mains.append(ba[pl.ds(x, 72, stride=12), :])
        t = roll(bb[pl.ds(x, 72, stride=12), :], 16 * x)
        tails[x // 8] = t if tails[x // 8] is None else tails[x // 8] + t
    terms = jnp.concatenate(mains + tails, axis=1)
    t_hi = terms.astype(BF16)
    t_lo = (terms - t_hi.astype(F32)).astype(BF16)
    gb = mm_nt(t_hi, spread_v[...]) + mm_nt(t_lo, spread_v[...])
    g0, g1, g2 = gb[:, 0:128], gb[:, 128:256], gb[:, 256:384]
    rest = jnp.concatenate([roll(g2[40:72], 64), jnp.zeros((8, 128), F32)], axis=0)
    packed = jnp.concatenate([g0, g1[64:72], g1[0:64], g2[0:40] + rest, jnp.zeros((8, 128), F32)], axis=0)
    for which in range(2):
        mine = jnp.where(band == which, packed, 0.0).astype(BF16)
        for t in range(12):
            pay[(which, *bias_place(t))] = mine[t * 16:(t + 1) * 16]
    rest_of = pl.ds(MAIN, CHUNKS - MAIN)
    cores.append(remote(pay.at[1 - core, rest_of], rc.at[rest_of], c_ss.at[1], c_rs.at[1], sibling))
    cores[1].start()

    for cp in cores:
        cp.wait_recv()
    scatter = []
    for d, j in enumerate(to_first + [group]):
        cur[j] = (pay[core, j].astype(F32) + rc[j].astype(F32)).astype(BF16)
        if d < 7:
            cp = remote(cur.at[j], ra.at[group], a_ss.at[d], a_rs.at[d], member(j))
            cp.start()
            scatter.append(cp)
    ra[group] = cur[group]

    dn = jnp.concatenate([mm_tn(d, wqkv_t[...]) for d in d_qkv_t], axis=0)
    m1 = jnp.sum(dn, axis=1, keepdims=True) * (1.0 / WIDTH)
    m2 = jnp.sum(dn * xhat, axis=1, keepdims=True) * (1.0 / WIDTH)
    gf = (cot_f + rdev * (dn - m1 - xhat * m2)).astype(BF16)
    gback[0:TOK, :] = gf
    ret_b[...] = mm(cells_v[SENT:2 * SENT, :], gf).astype(BF16)
    ret_to = [(lat_o, lon), (lat, east), (lat_o, east)]
    returns = [remote(ret_b.at[pl.ds(a, n)], gback.at[pl.ds(b, n)], r_ss.at[i], r_rs.at[i], ret_to[i])
               for i, (a, b, n) in enumerate(STRIPS)]
    for cp in returns:
        cp.start()

    def total(ref, n):
        acc = ref[0].astype(F32)
        for i in range(1, n):
            acc = acc + ref[i].astype(F32)
        return acc.astype(BF16)

    for cp in scatter:
        cp.wait_recv()
    ry[place2] = total(ra, 8)
    over_y = [remote(ry.at[place2], ry.at[place2], y_ss.at[i], y_rs.at[i], second(j))
              for i, j in enumerate(to_second)]
    for cp in over_y:
        cp.start()

    for cp in returns:
        cp.wait_recv()
    field_ref[...] = mm(moves_v[TOK:2 * TOK, :], gback[...]).astype(BF16)

    for cp in over_y:
        cp.wait_recv()
    rz[place3] = total(ry, 8)
    over_z = [remote(rz.at[place3], rz.at[place3], z_ss.at[i], z_rs.at[i], third(j))
              for i, j in enumerate(to_third)]
    for cp in over_z:
        cp.start()
    for cp in over_z:
        cp.wait_recv()

    fin[core, group] = total(rz, 4)
    gather = [remote(fin.at[core, group], fin.at[core, group], g_ss.at[i], g_rs.at[i], member(j))
              for i, j in enumerate(to_first)]
    for cp in gather:
        cp.start()
    final = []
    for i in (7, 6, 5, 4, 3, 2, 1, 0):
        if i < 7:
            gather[i].wait_recv()
        j = group if i == 7 else from_first[i]
        cp = remote(fin.at[core, j], fin.at[core, j], k_ss.at[i], k_rs.at[i], sibling)
        cp.start()
        final.append(cp)
    for cp in final:
        cp.wait_recv()
    for cp in halo + returns + cores + scatter + over_y + over_z + gather + final:
        cp.wait_send()


def unpack(field_in, fin, field_hbm, gqkv_hbm, gproj_hbm, gbias_hbm, gqkv_ref, gproj_ref, gbias_ref, sem):
    outs = [(field_in, field_hbm), (gqkv_ref, gqkv_hbm), (gproj_ref, gproj_hbm), (gbias_ref.at[pl.ds(0, 864)], gbias_hbm)]
    stores = [pltpu.make_async_copy(src, dst, sem.at[i]) for i, (src, dst) in enumerate(outs)]
    stores[0].start()
    token_scale = 147456.0 ** (-0.5)
    for i in range(ROWS_MAIN):
        r = slice(i * 16, (i + 1) * 16)
        row = [fin[main_place(i * COLS_MAIN + j)].astype(F32) * token_scale for j in range(COLS_MAIN)]
        for j in range(4):
            gqkv_ref[r, j * 128:(j + 1) * 128] = row[j]
        gqkv_ref[r, 512:576] = row[4][:, 0:64]
        gproj_ref[r, 0:128] = row[5]
        gproj_ref[r, 128:192] = row[4][:, 64:128]
    stores[1].start()
    stores[2].start()
    bias_rows = gbias_ref.reshape(2 * PAD, 23)
    for which in range(2):
        packed = jnp.concatenate([fin[(which, *bias_place(t))] for t in range(12)], axis=0).astype(F32)
        rest = packed[144:184]
        cols = [packed[0:72], jnp.concatenate([packed[80:144], packed[72:80]], axis=0),
                jnp.concatenate([rest, roll(rest[0:32], -64)], axis=0)]
        for g in range(3):
            for k in range(PACKS[g]):
                place = pl.ds(2 * (5 * g + k) + which, 72, stride=24)
                bias_rows[place, :] = roll(cols[g], -24 * k)[:, 0:23]
    stores[3].start()
    for cp in stores:
        cp.wait()


def body(grid_state, cotangent, mask_ids, earth_bias, qkv_weight, proj_weight):
    tables = [jnp.asarray(t) for t in build_tables()]
    vm = pltpu.VMEM
    dma = lambda n: pltpu.SemaphoreType.DMA((n,))
    tiles = lambda *n: vm((*n, 16, 128), BF16)
    scratch = [
        vm((TOK, WIDTH), BF16), vm((TOK, WIDTH), BF16), vm((6, 2, 24), jnp.int32),
        vm((PAD, 2, 23), F32), vm((192, 576), BF16), vm((192, 192), BF16),
        vm((2 * SENT, TOK), BF16), vm((2 * TOK, ALL), BF16), vm((TOK, 384), BF16),
        vm((384, 1792), BF16),
        vm((ALL, 384), BF16), vm((SENT, 384), BF16), vm((4, 16, 128), BF16),
        vm((PAD, 128), F32), vm((PAD, 128), F32), vm((PAD, 128), F32), vm((PAD, 128), F32),
        vm((ALL, WIDTH), BF16), vm((SENT, WIDTH), BF16), vm((576, WIDTH), BF16),
        tiles(2, CHUNKS, TILES), tiles(CHUNKS, TILES), tiles(CHUNKS, TILES), tiles(8, TILES), tiles(8, TILES), tiles(4, TILES),
        dma(10), dma(6), dma(6), dma(3), dma(3), dma(2), dma(2), dma(7), dma(7), dma(7), dma(7),
        dma(3), dma(3), dma(7), dma(7), dma(8), dma(8),
    ]
    any_space = pl.BlockSpec(memory_space=pl.ANY)
    in_vmem = pl.BlockSpec(memory_space=pltpu.VMEM)
    field, fin = pl.pallas_call(
        kernel,
        out_shape=(
            jax.ShapeDtypeStruct((TOK, WIDTH), BF16),
            jax.ShapeDtypeStruct((2, CHUNKS, TILES, 16, 128), BF16),
        ),
        in_specs=[any_space] * 10,
        out_specs=(in_vmem,) * 2,
        scratch_shapes=scratch,
        compiler_params=pltpu.CompilerParams(
            collective_id=0, has_side_effects=True, vmem_limit_bytes=48 * 2**20),
        name="window_backward",
    )(
        *[pltpu.with_memory_space_constraint(o, pltpu.HBM) for o in (grid_state.reshape(TOK, WIDTH), cotangent.reshape(TOK, WIDTH),
        mask_ids.transpose(1, 0, 2), earth_bias.transpose(1, 2, 3, 0, 4).reshape(864, 2, 23),
        qkv_weight, proj_weight, *tables)]
    )
    field, gqkv, gproj, gbias = pl.pallas_call(
        unpack,
        out_shape=(
            jax.ShapeDtypeStruct((TOK, WIDTH), BF16),
            jax.ShapeDtypeStruct((192, 576), F32),
            jax.ShapeDtypeStruct((192, 192), F32),
            jax.ShapeDtypeStruct((864, 2, 23), F32),
        ),
        in_specs=[in_vmem] * 2,
        out_specs=(any_space,) * 4,
        scratch_shapes=[vm((192, 576), F32), vm((192, 192), F32), vm((PAD, 2, 23), F32), dma(4)],
        compiler_params=pltpu.CompilerParams(vmem_limit_bytes=16 * 2**20),
        name="unpack",
    )(field, fin)
    gbias = gbias.reshape(6, 12, 12, 2, 23).transpose(3, 0, 1, 2, 4)
    return field.reshape(grid_state.shape), gqkv, gproj, gbias


def solution(mesh):
    placed = (
        P(None, "lat", "lon", None),
        P(None, "lat", "lon", None),
        P(None, "lat", "lon"),
        P(),
        P(),
        P(),
    )
    return jax.shard_map(
        body,
        mesh=mesh,
        in_specs=placed,
        out_specs=(P(None, "lat", "lon", None), P(), P(), P()),
        check_vma=False,
    )
```
